256 devices in a mesh: seq: 32 (over z, x), req: 8 (over y, core).
Axes of the slice: x: 4, y: 4, z: 8, core: 2. Of those that a mesh axis runs over, the one named last changes fastest.
Arguments:
- tokens: bfloat16 [64, 4, 2048], P('req'), may hold values from -6 to 6
- lengths: int32 [64], P('req'), may hold values from 1 to 2044, as said below
- cache_keys: bfloat16 [64, 2048, 2048], P('req', 'seq'), may hold values from -120 to 120
- cache_values: bfloat16 [64, 2048, 2048], P('req', 'seq'), may hold values from -6 to 6
- norm1_gain: float32 [2048], replicated, may hold values from 0.5 to 1.5
- norm1_bias: float32 [2048], replicated, may hold values from -1.75 to 1.75
- w_query: bfloat16 [2048, 2048], P('req', 'seq'), may hold values from -0.125 to 0.125
- b_query: float32 [2048], P('seq'), may hold values from -3 to 3
- w_key: bfloat16 [2048, 2048], P('req', 'seq'), may hold values from -0.125 to 0.125
- b_key: float32 [2048], P('seq'), may hold values from -3 to 3
- w_value: bfloat16 [2048, 2048], P('req', 'seq'), may hold values from -0.125 to 0.125
- b_value: float32 [2048], P('seq'), may hold values from -3 to 3
- w_out: bfloat16 [2048, 2048], P('req', 'seq'), may hold values from -0.125 to 0.125
- b_out: float32 [2048], P('seq'), may hold values from -3 to 3
- norm2_gain: float32 [2048], replicated, may hold values from 0.5 to 1.5
- norm2_bias: float32 [2048], replicated, may hold values from -1.75 to 1.75
- w_up: bfloat16 [2048, 8192], P('req', 'seq'), may hold values from -0.125 to 0.125
- b_up: float32 [8192], P('seq'), may hold values from -3 to 3
- w_down: bfloat16 [8192, 2048], P('seq', 'req'), may hold values from -0.0625 to 0.0625
- b_down: float32 [2048], replicated, may hold values from -3 to 3
Outputs:
- hidden_out: bfloat16 [64, 4, 2048], P('req')
- new_keys: bfloat16 [64, 2048, 2048], P('req', 'seq')
- new_values: bfloat16 [64, 2048, 2048], P('req', 'seq')
The draws below stay inside these ranges and needn't reach their ends.
Inputs may be any that keep to these rules, and one draw needn't show every extreme that they name: `lengths`: one request has exactly 2044 cached positions.
All inputs are finite; a program needn't handle non-finite values.
Results may differ from the reference program's by a relative error of at most 0.033.
Values may be sent and summed in bfloat16 or wider, within the bound.
A program may use at most 64 MiB of HBM per device.

```python
import jax
import jax.numpy as jnp
from jax import lax

D = 2048
HEADS = 16
HEAD = 128
FF = 8192
STEPS = 4
REQS = 64
CACHE = 2048


def draw_lengths(key, part):
    top = CACHE - STEPS
    first, second, third = jax.random.split(jax.random.fold_in(key, 11), 3)
    left = jax.random.randint(first, (REQS,), 0, top)
    right = jax.random.randint(second, (REQS,), 0, top)
    base = left * right // top + 1
    chosen = jax.random.randint(third, (), 0, REQS)
    return jnp.where(jnp.arange(REQS) == chosen, top, base).astype(jnp.int32)


def draw_cache_keys(key, part):
    first = jax.random.fold_in(jax.random.fold_in(key, 23), 0)
    values = jnp.clip(jax.random.normal(first, (REQS, CACHE, D), jnp.float32), -4.0, 4.0)
    return values.astype(jnp.bfloat16)


def block_scale(own_key, extent, cuts, low, high):
    def one(dim, shards_of):
        steps = jax.random.uniform(jax.random.fold_in(jax.random.fold_in(own_key, 6), dim), (shards_of,), jnp.float32, low / len(cuts), high / len(cuts))
        return jnp.repeat(jnp.exp(steps), extent[dim] // shards_of).reshape((-1,) + (1,) * (len(extent) - dim - 1))

    factor_of = one(*cuts[0])
    for cut in cuts[1:]:
        factor_of = factor_of * one(*cut)
    return factor_of


def scatter_about(rng, extent, width, reach, cuts=(), kind=jnp.bfloat16):
    result = jax.random.normal(rng, extent, jnp.float32) * width
    if len(cuts) > 0:
        result = block_scale(rng, extent, cuts, -0.22, 0.18) * result
    return jnp.clip(result, min=-reach, max=reach).astype(kind)


def setup_inputs(seed: int = 0) -> dict:
    key_of = jax.random.split(jax.random.key(seed), 21)
    return {
        "tokens": scatter_about(key_of[0], (REQS, STEPS, D), 1.0, 6.0, ((0, 8),)),
        "lengths": draw_lengths(jax.random.fold_in(key_of[20], 71), 0),
        "cache_keys": draw_cache_keys(jax.random.fold_in(key_of[20], 71), 0),
        "cache_values": scatter_about(key_of[3], (REQS, CACHE, D), 1.0, 6.0, ((0, 8), (1, 32))),
        "norm1_gain": jnp.clip(jax.random.uniform(key_of[4], (D,), jnp.float32, 0.5, 1.5), 0.5, 1.5),
        "norm1_bias": scatter_about(key_of[5], (D,), 0.3, 1.75, (), jnp.float32),
        "w_query": scatter_about(key_of[6], (D, D), D ** -0.5, 0.125, ((0, 8), (1, 32))),
        "b_query": scatter_about(key_of[7], (D,), 0.5, 3.0, ((0, 32),), jnp.float32),
        "w_key": scatter_about(key_of[8], (D, D), D ** -0.5, 0.125, ((0, 8), (1, 32))),
        "b_key": scatter_about(key_of[9], (D,), 0.5, 3.0, ((0, 32),), jnp.float32),
        "w_value": scatter_about(key_of[10], (D, D), D ** -0.5, 0.125, ((0, 8), (1, 32))),
        "b_value": scatter_about(key_of[11], (D,), 0.5, 3.0, ((0, 32),), jnp.float32),
        "w_out": scatter_about(key_of[12], (D, D), D ** -0.5, 0.125, ((0, 8), (1, 32))),
        "b_out": scatter_about(key_of[13], (D,), 0.5, 3.0, ((0, 32),), jnp.float32),
        "norm2_gain": jnp.clip(jax.random.uniform(key_of[14], (D,), jnp.float32, 0.5, 1.5), 0.5, 1.5),
        "norm2_bias": scatter_about(key_of[15], (D,), 0.3, 1.75, (), jnp.float32),
        "w_up": scatter_about(key_of[16], (D, FF), D ** -0.5, 0.125, ((0, 8), (1, 32))),
        "b_up": scatter_about(key_of[17], (FF,), 0.5, 3.0, ((0, 32),), jnp.float32),
        "w_down": scatter_about(key_of[18], (FF, D), FF ** -0.5, 0.0625, ((0, 32), (1, 8))),
        "b_down": scatter_about(key_of[19], (D,), 0.5, 3.0, (), jnp.float32),
    }


def layer_norm(values, gain, shift):
    center = values - lax.optimization_barrier(jnp.mean(values, axis=-1, keepdims=True))
    spread = lax.optimization_barrier(jnp.mean(center * center, axis=-1, keepdims=True))
    return center * lax.rsqrt(spread + 1e-05) * gain + shift

def reference(tokens, lengths, cache_keys, cache_values, norm1_gain, norm1_bias, w_query, b_query, w_key, b_key, w_value, b_value, w_out, b_out, norm2_gain, norm2_bias, w_up, b_up, w_down, b_down):
    residual = tokens.astype(jnp.float32)
    normed = layer_norm(residual, norm1_gain, norm1_bias).astype(jnp.bfloat16)
    query = (jnp.dot(normed, w_query, preferred_element_type=jnp.float32) + b_query).astype(jnp.bfloat16)
    key_rows = (jnp.dot(normed, w_key, preferred_element_type=jnp.float32) + b_key).astype(jnp.bfloat16)
    value_rows = (jnp.dot(normed, w_value, preferred_element_type=jnp.float32) + b_value).astype(jnp.bfloat16)
    position = jnp.arange(CACHE, dtype=jnp.int32)
    offsets = jnp.arange(STEPS, dtype=jnp.int32)
    factor = HEAD ** (-0.5)

    def one_request(items):
        keys, values, length, query_row, key_new, value_new = items
        for step in range(STEPS):
            hit = (position == length + step)[:, None]
            keys = jnp.where(hit, key_new[step][None, :], keys)
            values = jnp.where(hit, value_new[step][None, :], values)
        query_heads = query_row.reshape(STEPS, HEADS, HEAD).astype(jnp.float32)
        key_heads = keys.reshape(CACHE, HEADS, HEAD).astype(jnp.float32)
        value_heads = values.reshape(CACHE, HEADS, HEAD).astype(jnp.float32)
        scores = jnp.einsum('thd,shd->ths', query_heads, key_heads) * factor
        valid = position[None, None, :] <= (length + offsets)[:, None, None]
        masked = jnp.where(valid, scores, -1e+30)
        peak = lax.optimization_barrier(jnp.max(masked, axis=-1))
        expo = jnp.where(valid, jnp.exp(masked - peak[..., None]), 0.0)
        total = lax.optimization_barrier(jnp.sum(expo, axis=-1))
        probs = expo.astype(jnp.bfloat16).astype(jnp.float32)
        mixed = jnp.einsum('ths,shd->thd', probs, value_heads) / total[..., None]
        return (keys, values, mixed.reshape(STEPS, D).astype(jnp.bfloat16))
    new_keys, new_values, attn = lax.map(one_request, (cache_keys, cache_values, lengths, query, key_rows, value_rows))
    projected = (jnp.dot(attn, w_out, preferred_element_type=jnp.float32) + b_out).astype(jnp.bfloat16)
    mid = residual + projected.astype(jnp.float32)
    normed2 = layer_norm(mid, norm2_gain, norm2_bias).astype(jnp.bfloat16)
    hidden = jax.nn.gelu(jnp.dot(normed2, w_up, preferred_element_type=jnp.float32) + b_up, approximate=False).astype(jnp.bfloat16)
    hidden_out = (mid + jnp.dot(hidden, w_down, preferred_element_type=jnp.float32) + b_down).astype(jnp.bfloat16)
    return (hidden_out, new_keys, new_values)
```

```python
import functools

import jax
import jax.numpy as jnp
from jax import lax
from jax.experimental import pallas as pl
from jax.experimental.pallas import tpu as pltpu
from jax.sharding import PartitionSpec as P

HEADS = 16
HEAD = 128
SEQ = 32
REQ = 8
ROWS = 32
WIDTH = 2048
SPOTS = 512
MESH = pl.DeviceIdType.MESH
F32 = jnp.float32
BF16 = jnp.bfloat16
NT = (((1,), (1,)), ((), ()))


def layer_norm(values, gain, shift):
    center = values - jnp.mean(values, axis=-1, keepdims=True)
    spread = jnp.mean(center * center, axis=-1, keepdims=True)
    return center * lax.rsqrt(spread + 1e-05) * gain + shift


def far_first(i):
    a, b = i // 4, lax.rem(i, 4)
    dz = 4 + ((a + 1) // 2) * (1 - 2 * lax.rem(a, 2))
    dx = 2 + ((b + 1) // 2) * (1 - 2 * lax.rem(b, 2))
    return dz, dx


def unfold(slots, j):
    first = slots[2 * j].astype(F32)
    second = slots[2 * j + 1].astype(F32)
    low = lax.broadcasted_iota(jnp.int32, (16, 128), 1) < 64
    top = jnp.where(low, first, pltpu.roll(second, 64, 1))
    bottom = jnp.where(low, pltpu.roll(first, 64, 1), second)
    return jnp.concatenate([top, bottom], axis=0)


def kernel(
    lengths,
    tokens,
    cache_keys,
    cache_values,
    gain1,
    bias1,
    wq,
    bq,
    wk,
    bk,
    wv,
    bv,
    wo,
    bo,
    gain2,
    bias2,
    wu,
    bu,
    wd,
    bd,
    out,
    out_keys,
    out_values,
    x_buf,
    n_buf,
    k_buf,
    v_buf,
    wq_g,
    wkvo_g,
    wu_g,
    wd_g,
    q_g,
    kv_g,
    p_s,
    p_g,
    t_s,
    t_g,
    a_g,
    o_g,
    f_s,
    f_g,
    h_g,
    load_sem,
    store_sem,
    send_sem,
    recv_sem,
):
    s = lax.axis_index("seq")
    r = lax.axis_index("req")
    z, x = s // 4, lax.rem(s, 4)
    y, core = r // 2, lax.rem(r, 2)
    sibling = y * 2 + 1 - core
    head, half = s // 2, lax.rem(s, 2)

    barrier = pltpu.get_barrier_semaphore()

    def far(i):
        dz, dx = far_first(i)
        return lax.rem(z + dz, 8) * 4 + lax.rem(x + dx, 4)

    def greet_seq(i, _):
        pl.semaphore_signal(barrier, inc=1, device_id=(far(i), r), device_id_type=MESH)
        return 0

    def greet_req(k, _):
        pl.semaphore_signal(barrier, inc=1, device_id=(s, lax.rem(r + k, REQ)), device_id_type=MESH)
        return 0

    lax.fori_loop(0, SEQ - 1, greet_seq, 0)
    lax.fori_loop(1, REQ, greet_req, 0)

    loads = [
        (wq, wq_g.at[r]),
        (wk, wkvo_g.at[r, 0]),
        (wv, wkvo_g.at[r, 1]),
        (wo, wkvo_g.at[r, 2]),
        (wu, wu_g.at[r]),
        (wd, wd_g.at[r]),
        (cache_keys, k_buf),
        (cache_values, v_buf),
    ]
    loads = [pltpu.make_async_copy(a, b, load_sem.at[i]) for i, (a, b) in enumerate(loads)]
    for load in loads:
        load.start()

    for i in range(8):
        x_buf[4 * i : 4 * i + 4, :] = tokens[i].astype(F32)
    n_buf[...] = layer_norm(x_buf[...], gain1[...], bias1[...]).astype(BF16)

    def send(src, dst, phase, device):
        pltpu.make_async_remote_copy(
            src, dst, send_sem.at[phase], recv_sem.at[phase], device_id=device, device_id_type=MESH
        ).start()

    def received(ref, phase):
        pltpu.make_async_remote_copy(
            ref, ref, send_sem.at[phase], recv_sem.at[phase], device_id=(s, sibling), device_id_type=MESH
        ).wait_recv()

    def sent(ref, phase):
        pltpu.make_async_remote_copy(
            ref, ref, send_sem.at[phase], recv_sem.at[phase], device_id=(s, sibling), device_id_type=MESH
        ).wait_send()

    def spread(src, slots, phase):
        def one(i, _):
            send(src, slots.at[s], phase, (far(i), r))
            return 0

        lax.fori_loop(0, SEQ - 1, one, 0)

    def along_y(buf, phase):
        for k in (2, 1, 3):
            send(buf.at[r], buf.at[r], phase, (s, lax.rem(y + k, 4) * 2 + core))

    def across(buf, phase, own):
        for k in (0,) if own else (1, 3, 2):
            block = lax.rem(y + k, 4) * 2 + core
            send(buf.at[block], buf.at[block], phase, (s, sibling))

    for load in loads[:4]:
        load.wait()
    pl.semaphore_wait(barrier, SEQ - 1 + REQ - 1)

    along_y(wq_g, 0)
    across(wq_g, 1, True)
    along_y(wkvo_g, 2)
    across(wkvo_g, 3, True)
    received(wq_g.at[pl.ds(0, 3)], 0)
    across(wq_g, 1, False)
    received(wq_g.at[pl.ds(0, 4)], 1)

    low = lax.broadcasted_iota(jnp.int32, (16, 128), 1) < 64

    total = jnp.zeros((ROWS, 128), F32)
    for k in range(REQ):
        weight = wq_g[k]
        total += lax.dot_general(
            n_buf[:, 256 * k : 256 * k + 256],
            jnp.concatenate([weight, weight], axis=0),
            NT,
            preferred_element_type=F32,
        )
    total += jnp.concatenate([bq[...], bq[...]], axis=1)
    q_g[s] = jnp.where(low, total[:16], total[16:]).astype(BF16)
    spread(q_g.at[s], q_g, 4)

    received(wkvo_g.at[pl.ds(0, 3)], 2)
    across(wkvo_g, 3, False)
    for load in loads[4:]:
        load.wait()
    received(wkvo_g.at[pl.ds(0, 4)], 3)
    total = jnp.zeros((ROWS, 128), F32)
    for k in range(REQ):
        total += lax.dot_general(
            n_buf[:, 256 * k : 256 * k + 256],
            wkvo_g[k, 0:2].reshape(128, 256),
            NT,
            preferred_element_type=F32,
        )
    total += jnp.concatenate([bk[...], bv[...]], axis=1)
    kv_g[s, 0] = jnp.where(low, total[:16], pltpu.roll(total[16:], 64, 1)).astype(BF16)
    kv_g[s, 1] = jnp.where(low, pltpu.roll(total[:16], 64, 1), total[16:]).astype(BF16)
    spread(kv_g.at[s], kv_g, 5)

    along_y(wu_g, 6)
    across(wu_g, 7, True)
    along_y(wd_g, 8)
    across(wd_g, 9, True)

    scale = HEAD**-0.5
    row = lax.broadcasted_iota(jnp.int32, (ROWS, SPOTS), 0)
    col = lax.broadcasted_iota(jnp.int32, (ROWS, SPOTS), 1)
    limit = jnp.zeros((ROWS, SPOTS), jnp.int32)
    for k in range(8):
        limit = jnp.where((row >> 2) == k, lengths[k], limit)
    valid = ((row >> 2) == (col >> 6)) & ((col & 63) + s * 64 < limit)
    lane = lax.broadcasted_iota(jnp.int32, (ROWS, 128), 1)

    received(q_g.at[pl.ds(0, SEQ - 1)], 4)

    def one_head(j, stats):
        query = unfold(q_g, j).astype(BF16)
        columns = pl.ds(pl.multiple_of(j * 128, 128), 128)
        scores = lax.dot_general(query, k_buf[:, columns], NT, preferred_element_type=F32) * scale
        scores = jnp.where(valid, scores, -1e30)
        peak = jnp.maximum(jnp.max(scores, axis=1, keepdims=True), -1e20)
        expo = jnp.exp(scores - peak)
        amount = jnp.sum(expo, axis=1, keepdims=True)
        part = jnp.dot(expo.astype(BF16), v_buf[:, columns], preferred_element_type=F32)
        p_s[2 * j] = part[:16].astype(BF16)
        p_s[2 * j + 1] = part[16:].astype(BF16)
        return jnp.where(lane == j, peak, jnp.where(lane == j + 16, amount, stats))

    def four_heads(g, stats):
        for j in range(4):
            stats = one_head(4 * g + j, stats)
        return stats

    stats = lax.fori_loop(0, 4, four_heads, jnp.zeros((ROWS, 128), F32))
    turned = stats.T
    turned = jnp.concatenate([turned[:16], turned[16:32], jnp.zeros((16, 64), F32)], axis=1)
    for j in range(HEADS):
        t_s[j] = turned[j : j + 1]

    def share(i, _):
        peer = far(i)
        send(p_s.at[peer], p_g.at[s], 10, (peer, r))
        send(t_s.at[peer // 2], t_g.at[s], 11, (peer, r))
        return 0

    lax.fori_loop(0, SEQ - 1, share, 0)
    p_g[s] = p_s[s]
    t_g[s] = t_s[head]

    received(kv_g.at[pl.ds(0, SEQ - 1)], 5)
    spot = lax.broadcasted_iota(jnp.int32, (SPOTS, ROWS), 0)
    new = lax.broadcasted_iota(jnp.int32, (SPOTS, ROWS), 1)
    start = jnp.zeros((SPOTS, ROWS), jnp.int32)
    for k in range(8):
        start = jnp.where((new >> 2) == k, lengths[k], start)
    hit = ((new >> 2) == (spot >> 6)) & ((spot & 63) + s * 64 == start + (new & 3))
    pick = jnp.where(hit, 1.0, 0.0)
    changed = jnp.max(pick, axis=1, keepdims=True) > 0.5
    pick = pick.astype(BF16)

    def renew(which, buf):
        def one(j, _):
            columns = pl.ds(pl.multiple_of(j * 128, 128), 128)
            rows = unfold(kv_g.at[:, which], j).astype(BF16)
            fresh = jnp.dot(pick, rows, preferred_element_type=F32)
            buf[:, columns] = jnp.where(changed, fresh, buf[:, columns].astype(F32)).astype(BF16)
            return 0

        lax.fori_loop(0, HEADS, one, 0)

    renew(0, k_buf)
    store_keys = pltpu.make_async_copy(k_buf, out_keys, store_sem.at[0])
    store_keys.start()

    def mine(slots):
        return unfold(slots, head)

    query = mine(q_g)
    query = jnp.where(half == 0, query[:16], query[16:]).astype(BF16)
    fresh_keys = mine(kv_g.at[:, 0]).astype(BF16)
    fresh_values = mine(kv_g.at[:, 1]).astype(BF16)
    row = lax.broadcasted_iota(jnp.int32, (16, ROWS), 0) + half * 16
    col = lax.broadcasted_iota(jnp.int32, (16, ROWS), 1)
    scores = lax.dot_general(query, fresh_keys, NT, preferred_element_type=F32) * scale
    scores = jnp.where(((row >> 2) == (col >> 2)) & ((col & 3) <= (row & 3)), scores, -1e30)
    peak_new = jnp.max(scores, axis=1, keepdims=True)
    expo = jnp.exp(scores - peak_new)
    total_new = jnp.sum(expo, axis=1, keepdims=True)
    part_new = jnp.dot(expo.astype(BF16), fresh_values, preferred_element_type=F32)

    received(t_g.at[pl.ds(0, SEQ - 1)], 11)
    turned = t_g[...].reshape(SEQ, 128).T
    peaks = jnp.where(half == 0, turned[0:16], turned[16:32])
    totals = jnp.where(half == 0, turned[32:48], turned[48:64])
    peak = jnp.maximum(jnp.max(peaks, axis=1, keepdims=True), peak_new)
    share_new = jnp.exp(peak_new - peak)
    shares = jnp.exp(peaks - peak)
    total = jnp.sum(shares * totals, axis=1, keepdims=True) + share_new * total_new
    received(p_g.at[pl.ds(0, SEQ - 1)], 10)
    mixed = share_new * part_new
    for k in range(SEQ):
        mixed += shares[:, k : k + 1] * p_g[k].astype(F32)
    a_g[s] = (mixed / total).astype(BF16)
    spread(a_g.at[s], a_g, 12)

    received(wu_g.at[pl.ds(0, 3)], 6)
    across(wu_g, 7, False)
    received(wd_g.at[pl.ds(0, 3)], 8)
    across(wd_g, 9, False)
    renew(1, v_buf)
    store_values = pltpu.make_async_copy(v_buf, out_values, store_sem.at[1])
    store_values.start()

    received(a_g.at[pl.ds(0, SEQ - 1)], 12)
    total = jnp.zeros((ROWS, 128), F32)
    for k in range(REQ):
        left = jnp.concatenate([a_g[4 * k], a_g[4 * k + 1]], axis=0)
        right = jnp.concatenate([a_g[4 * k + 2], a_g[4 * k + 3]], axis=0)
        weight = wkvo_g[k, 2]
        total += lax.dot_general(
            jnp.concatenate([left, right], axis=1),
            jnp.concatenate([weight, weight], axis=0),
            NT,
            preferred_element_type=F32,
        )
    total += jnp.concatenate([bo[...], bo[...]], axis=1)
    o_g[s] = jnp.where(low, total[:16], total[16:]).astype(BF16)
    spread(o_g.at[s], o_g, 13)
    received(wu_g.at[pl.ds(0, 4)], 7)
    received(wd_g.at[pl.ds(0, 4)], 9)
    received(o_g.at[pl.ds(0, SEQ - 1)], 13)

    for j in range(HEADS):
        x_buf[:, 128 * j : 128 * j + 128] += unfold(o_g, j)
    n_buf[...] = layer_norm(x_buf[...], gain2[...], bias2[...]).astype(BF16)
    total = jnp.zeros((ROWS, 256), F32)
    for k in range(REQ):
        total += jnp.dot(n_buf[:, 256 * k : 256 * k + 256], wu_g[k], preferred_element_type=F32)
    total += bu[...]
    hidden = (0.5 * total * (1.0 + lax.erf(total * (0.5**0.5)))).astype(BF16)
    for k in range(REQ):
        feed = jnp.dot(hidden, wd_g[k], preferred_element_type=F32).astype(BF16)
        f_s[4 * k] = feed[:16, :128]
        f_s[4 * k + 1] = feed[16:, :128]
        f_s[4 * k + 2] = feed[:16, 128:]
        f_s[4 * k + 3] = feed[16:, 128:]

    def scatter(i, _):
        peer = far(i)
        send(f_s.at[peer], f_g.at[s], 14, (peer, r))
        return 0

    lax.fori_loop(0, SEQ - 1, scatter, 0)
    f_g[s] = f_s[s]
    columns = pl.ds(pl.multiple_of(head * 128, 128), 128)
    mid = x_buf[pl.ds(pl.multiple_of(half * 16, 16), 16), columns] + bd[:, columns]
    received(f_g.at[pl.ds(0, SEQ - 1)], 14)
    summed = f_g[0].astype(F32)
    for k in range(1, SEQ):
        summed += f_g[k].astype(F32)
    h_g[s] = (mid + summed).astype(BF16)
    spread(h_g.at[s], h_g, 15)

    store_keys.wait()
    store_values.wait()
    for buf, phase in ((wq_g, 0), (wkvo_g, 2), (wu_g, 6), (wd_g, 8)):
        sent(buf.at[pl.ds(0, 3)], phase)
        sent(buf.at[pl.ds(0, 4)], phase + 1)
    for buf, phase in ((q_g, 4), (kv_g, 5), (p_g, 10), (t_g, 11), (a_g, 12), (o_g, 13), (f_g, 14)):
        sent(buf.at[pl.ds(0, SEQ - 1)], phase)
    received(h_g.at[pl.ds(0, SEQ - 1)], 15)
    for j in range(HEADS):
        out[0:16, 128 * j : 128 * j + 128] = h_g[2 * j]
        out[16:32, 128 * j : 128 * j + 128] = h_g[2 * j + 1]
    sent(h_g.at[pl.ds(0, SEQ - 1)], 15)


def body(
    tokens,
    lengths,
    cache_keys,
    cache_values,
    norm1_gain,
    norm1_bias,
    w_query,
    b_query,
    w_key,
    b_key,
    w_value,
    b_value,
    w_out,
    b_out,
    norm2_gain,
    norm2_bias,
    w_up,
    b_up,
    w_down,
    b_down,
):
    vmem = pl.BlockSpec(memory_space=pltpu.VMEM)
    smem = pl.BlockSpec(memory_space=pltpu.SMEM)
    anywhere = pl.BlockSpec(memory_space=pl.ANY)

    def line(v):
        return v.reshape(1, -1)

    slots = pltpu.VMEM((SEQ, 16, 128), BF16)
    hidden_out, new_keys, new_values = pl.pallas_call(
        kernel,
        out_shape=(
            jax.ShapeDtypeStruct((ROWS, WIDTH), BF16),
            jax.ShapeDtypeStruct((SPOTS, WIDTH), BF16),
            jax.ShapeDtypeStruct((SPOTS, WIDTH), BF16),
        ),
        in_specs=[smem, vmem, anywhere, anywhere, vmem, vmem]
        + [anywhere, vmem] * 4
        + [vmem, vmem, anywhere, vmem, anywhere, vmem],
        out_specs=(vmem, anywhere, anywhere),
        scratch_shapes=[
            pltpu.VMEM((ROWS, WIDTH), F32),
            pltpu.VMEM((ROWS, WIDTH), BF16),
            pltpu.VMEM((SPOTS, WIDTH), BF16),
            pltpu.VMEM((SPOTS, WIDTH), BF16),
            pltpu.VMEM((REQ, 64, 256), BF16),
            pltpu.VMEM((REQ, 3, 64, 256), BF16),
            pltpu.VMEM((REQ, 256, 256), BF16),
            pltpu.VMEM((REQ, 256, 256), BF16),
            slots,
            pltpu.VMEM((SEQ, 2, 16, 128), BF16),
            slots,
            slots,
            pltpu.VMEM((HEADS, 1, 128), F32),
            pltpu.VMEM((SEQ, 1, 128), F32),
            slots,
            slots,
            slots,
            slots,
            slots,
            pltpu.SemaphoreType.DMA((8,)),
            pltpu.SemaphoreType.DMA((2,)),
            pltpu.SemaphoreType.DMA((16,)),
            pltpu.SemaphoreType.DMA((16,)),
        ],
        compiler_params=pltpu.CompilerParams(
            collective_id=0, has_side_effects=True, vmem_limit_bytes=40 * 1024 * 1024
        ),
        cost_estimate=pl.CostEstimate(flops=500_000_000, bytes_accessed=9_000_000, transcendentals=300_000),
    )(
        lengths,
        tokens,
        cache_keys.reshape(SPOTS, WIDTH),
        cache_values.reshape(SPOTS, WIDTH),
        line(norm1_gain),
        line(norm1_bias),
        w_query.T,
        line(b_query),
        w_key.T,
        line(b_key),
        w_value.T,
        line(b_value),
        w_out.T,
        line(b_out),
        line(norm2_gain),
        line(norm2_bias),
        w_up,
        line(b_up),
        w_down,
        line(b_down),
    )
    return (
        hidden_out.reshape(8, 4, WIDTH),
        new_keys.reshape(8, 64, WIDTH),
        new_values.reshape(8, 64, WIDTH),
    )


def solution(mesh):
    in_specs = (
        P("req", None, None),
        P("req"),
        P("req", "seq", None),
        P("req", "seq", None),
        P(),
        P(),
        P("req", "seq"),
        P("seq"),
        P("req", "seq"),
        P("seq"),
        P("req", "seq"),
        P("seq"),
        P("req", "seq"),
        P("seq"),
        P(),
        P(),
        P("req", "seq"),
        P("seq"),
        P("seq", "req"),
        P(),
    )
    out_specs = (P("req", None, None), P("req", "seq", None), P("req", "seq", None))
    return jax.shard_map(body, mesh=mesh, in_specs=in_specs, out_specs=out_specs, check_vma=False)
```

```python
import functools

import jax
import jax.numpy as jnp
from jax import lax
from jax.experimental import pallas as pl
from jax.experimental.pallas import tpu as pltpu
from jax.sharding import PartitionSpec as P

HEADS = 16
HEAD = 128
SEQ = 32
REQ = 8
ROWS = 32
WIDTH = 2048
SPOTS = 512
MESH = pl.DeviceIdType.MESH
F32 = jnp.float32
BF16 = jnp.bfloat16
NT = (((1,), (1,)), ((), ()))


def layer_norm(values, gain, shift):
    center = values - jnp.mean(values, axis=-1, keepdims=True)
    spread = jnp.mean(center * center, axis=-1, keepdims=True)
    return center * lax.rsqrt(spread + 1e-05) * gain + shift


def far_first(i):
    a, b = i // 4, lax.rem(i, 4)
    dz = 4 + ((a + 1) // 2) * (1 - 2 * lax.rem(a, 2))
    dx = 2 + ((b + 1) // 2) * (1 - 2 * lax.rem(b, 2))
    return dz, dx


def unfold(slots, j):
    first = slots[2 * j].astype(F32)
    second = slots[2 * j + 1].astype(F32)
    low = lax.broadcasted_iota(jnp.int32, (16, 128), 1) < 64
    top = jnp.where(low, first, pltpu.roll(second, 64, 1))
    bottom = jnp.where(low, pltpu.roll(first, 64, 1), second)
    return jnp.concatenate([top, bottom], axis=0)


def kernel(
    lengths,
    tokens,
    cache_keys,
    cache_values,
    gain1,
    bias1,
    wq,
    bq,
    wk,
    bk,
    wv,
    bv,
    wo,
    bo,
    gain2,
    bias2,
    wu,
    bu,
    wd,
    bd,
    out,
    out_keys,
    out_values,
    x_buf,
    n_buf,
    k_buf,
    v_buf,
    lengths_s,
    tokens_s,
    gain1_s,
    bias1_s,
    bq_s,
    bk_s,
    bv_s,
    bo_s,
    gain2_s,
    bias2_s,
    bu_s,
    bd_s,
    wq_g,
    wkvo_g,
    wu_g,
    wd_g,
    q_g,
    kv_g,
    p_s,
    p_g,
    t_s,
    t_g,
    a_g,
    o_g,
    f_s,
    f_g,
    h_g,
    load_sem,
    store_sem,
    send_sem,
    recv_sem,
):
    s = lax.axis_index("seq")
    r = lax.axis_index("req")
    z, x = s // 4, lax.rem(s, 4)
    y, core = r // 2, lax.rem(r, 2)
    sibling = y * 2 + 1 - core
    head, half = s // 2, lax.rem(s, 2)

    barrier = pltpu.get_barrier_semaphore()

    def far(i):
        dz, dx = far_first(i)
        return lax.rem(z + dz, 8) * 4 + lax.rem(x + dx, 4)

    def greet_seq(i, _):
        pl.semaphore_signal(barrier, inc=1, device_id=(far(i), r), device_id_type=MESH)
        return 0

    def greet_req(k, _):
        pl.semaphore_signal(barrier, inc=1, device_id=(s, lax.rem(r + k, REQ)), device_id_type=MESH)
        return 0

    lax.fori_loop(0, SEQ - 1, greet_seq, 0)
    lax.fori_loop(1, REQ, greet_req, 0)

    loads = [
        (tokens, tokens_s),
        (gain1, gain1_s),
        (bias1, bias1_s),
        (wq, wq_g.at[r]),
        (wk, wkvo_g.at[r, 0]),
        (wv, wkvo_g.at[r, 1]),
        (wo, wkvo_g.at[r, 2]),
        (bq, bq_s),
        (bk, bk_s),
        (bv, bv_s),
        (bo, bo_s),
        (lengths, lengths_s),
        (wu, wu_g.at[r]),
        (wd, wd_g.at[r]),
        (gain2, gain2_s),
        (bias2, bias2_s),
        (bu, bu_s),
        (bd, bd_s),
        (cache_keys, k_buf),
        (cache_values, v_buf),
    ]
    loads = [pltpu.make_async_copy(a, b, load_sem.at[i]) for i, (a, b) in enumerate(loads)]
    for load in loads:
        load.start()

    for load in loads[:3]:
        load.wait()
    for i in range(8):
        x_buf[4 * i : 4 * i + 4, :] = tokens_s[i].astype(F32)
    n_buf[...] = layer_norm(x_buf[...], gain1_s[...], bias1_s[...]).astype(BF16)

    def send(src, dst, phase, device):
        pltpu.make_async_remote_copy(
            src, dst, send_sem.at[phase], recv_sem.at[phase], device_id=device, device_id_type=MESH
        ).start()

    def received(ref, phase):
        pltpu.make_async_remote_copy(
            ref, ref, send_sem.at[phase], recv_sem.at[phase], device_id=(s, sibling), device_id_type=MESH
        ).wait_recv()

    def sent(ref, phase):
        pltpu.make_async_remote_copy(
            ref, ref, send_sem.at[phase], recv_sem.at[phase], device_id=(s, sibling), device_id_type=MESH
        ).wait_send()

    def spread(src, slots, phase):
        def one(i, _):
            send(src, slots.at[s], phase, (far(i), r))
            return 0

        lax.fori_loop(0, SEQ - 1, one, 0)

    def along_y(buf, phase):
        for k in (2, 1, 3):
            send(buf.at[r], buf.at[r], phase, (s, lax.rem(y + k, 4) * 2 + core))

    def across(buf, phase, own):
        for k in (0,) if own else (1, 3, 2):
            block = lax.rem(y + k, 4) * 2 + core
            send(buf.at[block], buf.at[block], phase, (s, sibling))

    for load in loads[3:12]:
        load.wait()
    pl.semaphore_wait(barrier, SEQ - 1 + REQ - 1)

    along_y(wq_g, 0)
    across(wq_g, 1, True)
    along_y(wkvo_g, 2)
    across(wkvo_g, 3, True)
    received(wq_g.at[pl.ds(0, 3)], 0)
    across(wq_g, 1, False)
    received(wq_g.at[pl.ds(0, 4)], 1)

    low = lax.broadcasted_iota(jnp.int32, (16, 128), 1) < 64

    total = jnp.zeros((ROWS, 128), F32)
    for k in range(REQ):
        weight = wq_g[k]
        total += lax.dot_general(
            n_buf[:, 256 * k : 256 * k + 256],
            jnp.concatenate([weight, weight], axis=0),
            NT,
            preferred_element_type=F32,
        )
    total += jnp.concatenate([bq_s[...], bq_s[...]], axis=1)
    q_g[s] = jnp.where(low, total[:16], total[16:]).astype(BF16)
    spread(q_g.at[s], q_g, 4)

    received(wkvo_g.at[pl.ds(0, 3)], 2)
    across(wkvo_g, 3, False)
    for load in loads[12:]:
        load.wait()
    received(wkvo_g.at[pl.ds(0, 4)], 3)
    total = jnp.zeros((ROWS, 128), F32)
    for k in range(REQ):
        total += lax.dot_general(
            n_buf[:, 256 * k : 256 * k + 256],
            wkvo_g[k, 0:2].reshape(128, 256),
            NT,
            preferred_element_type=F32,
        )
    total += jnp.concatenate([bk_s[...], bv_s[...]], axis=1)
    kv_g[s, 0] = jnp.where(low, total[:16], pltpu.roll(total[16:], 64, 1)).astype(BF16)
    kv_g[s, 1] = jnp.where(low, pltpu.roll(total[:16], 64, 1), total[16:]).astype(BF16)
    spread(kv_g.at[s], kv_g, 5)

    along_y(wu_g, 6)
    across(wu_g, 7, True)
    along_y(wd_g, 8)
    across(wd_g, 9, True)

    scale = HEAD**-0.5
    row = lax.broadcasted_iota(jnp.int32, (ROWS, SPOTS), 0)
    col = lax.broadcasted_iota(jnp.int32, (ROWS, SPOTS), 1)
    limit = jnp.zeros((ROWS, SPOTS), jnp.int32)
    for k in range(8):
        limit = jnp.where((row >> 2) == k, lengths_s[k], limit)
    valid = ((row >> 2) == (col >> 6)) & ((col & 63) + s * 64 < limit)
    lane = lax.broadcasted_iota(jnp.int32, (ROWS, 128), 1)

    received(q_g.at[pl.ds(0, SEQ - 1)], 4)

    def one_head(j, stats):
        query = unfold(q_g, j).astype(BF16)
        columns = pl.ds(pl.multiple_of(j * 128, 128), 128)
        scores = lax.dot_general(query, k_buf[:, columns], NT, preferred_element_type=F32) * scale
        scores = jnp.where(valid, scores, -1e30)
        peak = jnp.maximum(jnp.max(scores, axis=1, keepdims=True), -1e20)
        expo = jnp.exp(scores - peak)
        amount = jnp.sum(expo, axis=1, keepdims=True)
        part = jnp.dot(expo.astype(BF16), v_buf[:, columns], preferred_element_type=F32)
        p_s[2 * j] = part[:16].astype(BF16)
        p_s[2 * j + 1] = part[16:].astype(BF16)
        return jnp.where(lane == j, peak, jnp.where(lane == j + 16, amount, stats))

    def four_heads(g, stats):
        for j in range(4):
            stats = one_head(4 * g + j, stats)
        return stats

    stats = lax.fori_loop(0, 4, four_heads, jnp.zeros((ROWS, 128), F32))
    turned = stats.T
    turned = jnp.concatenate([turned[:16], turned[16:32], jnp.zeros((16, 64), F32)], axis=1)
    for j in range(HEADS):
        t_s[j] = turned[j : j + 1]

    def share(i, _):
        peer = far(i)
        send(p_s.at[peer], p_g.at[s], 10, (peer, r))
        send(t_s.at[peer // 2], t_g.at[s], 11, (peer, r))
        return 0

    lax.fori_loop(0, SEQ - 1, share, 0)
    p_g[s] = p_s[s]
    t_g[s] = t_s[head]

    received(kv_g.at[pl.ds(0, SEQ - 1)], 5)
    spot = lax.broadcasted_iota(jnp.int32, (SPOTS, ROWS), 0)
    new = lax.broadcasted_iota(jnp.int32, (SPOTS, ROWS), 1)
    start = jnp.zeros((SPOTS, ROWS), jnp.int32)
    for k in range(8):
        start = jnp.where((new >> 2) == k, lengths_s[k], start)
    hit = ((new >> 2) == (spot >> 6)) & ((spot & 63) + s * 64 == start + (new & 3))
    pick = jnp.where(hit, 1.0, 0.0)
    changed = jnp.max(pick, axis=1, keepdims=True) > 0.5
    pick = pick.astype(BF16)

    def renew(which, buf):
        def one(j, _):
            columns = pl.ds(pl.multiple_of(j * 128, 128), 128)
            rows = unfold(kv_g.at[:, which], j).astype(BF16)
            fresh = jnp.dot(pick, rows, preferred_element_type=F32)
            buf[:, columns] = jnp.where(changed, fresh, buf[:, columns].astype(F32)).astype(BF16)
            return 0

        lax.fori_loop(0, HEADS, one, 0)

    renew(0, k_buf)
    store_keys = pltpu.make_async_copy(k_buf, out_keys, store_sem.at[0])
    store_keys.start()

    def mine(slots):
        return unfold(slots, head)

    query = mine(q_g)
    query = jnp.where(half == 0, query[:16], query[16:]).astype(BF16)
    fresh_keys = mine(kv_g.at[:, 0]).astype(BF16)
    fresh_values = mine(kv_g.at[:, 1]).astype(BF16)
    row = lax.broadcasted_iota(jnp.int32, (16, ROWS), 0) + half * 16
    col = lax.broadcasted_iota(jnp.int32, (16, ROWS), 1)
    scores = lax.dot_general(query, fresh_keys, NT, preferred_element_type=F32) * scale
    scores = jnp.where(((row >> 2) == (col >> 2)) & ((col & 3) <= (row & 3)), scores, -1e30)
    peak_new = jnp.max(scores, axis=1, keepdims=True)
    expo = jnp.exp(scores - peak_new)
    total_new = jnp.sum(expo, axis=1, keepdims=True)
    part_new = jnp.dot(expo.astype(BF16), fresh_values, preferred_element_type=F32)

    received(t_g.at[pl.ds(0, SEQ - 1)], 11)
    turned = t_g[...].reshape(SEQ, 128).T
    peaks = jnp.where(half == 0, turned[0:16], turned[16:32])
    totals = jnp.where(half == 0, turned[32:48], turned[48:64])
    peak = jnp.maximum(jnp.max(peaks, axis=1, keepdims=True), peak_new)
    share_new = jnp.exp(peak_new - peak)
    shares = jnp.exp(peaks - peak)
    total = jnp.sum(shares * totals, axis=1, keepdims=True) + share_new * total_new
    received(p_g.at[pl.ds(0, SEQ - 1)], 10)
    mixed = share_new * part_new
    for k in range(SEQ):
        mixed += shares[:, k : k + 1] * p_g[k].astype(F32)
    a_g[s] = (mixed / total).astype(BF16)
    spread(a_g.at[s], a_g, 12)

    received(wu_g.at[pl.ds(0, 3)], 6)
    across(wu_g, 7, False)
    received(wd_g.at[pl.ds(0, 3)], 8)
    across(wd_g, 9, False)
    renew(1, v_buf)
    store_values = pltpu.make_async_copy(v_buf, out_values, store_sem.at[1])
    store_values.start()

    received(a_g.at[pl.ds(0, SEQ - 1)], 12)
    total = jnp.zeros((ROWS, 128), F32)
    for k in range(REQ):
        left = jnp.concatenate([a_g[4 * k], a_g[4 * k + 1]], axis=0)
        right = jnp.concatenate([a_g[4 * k + 2], a_g[4 * k + 3]], axis=0)
        weight = wkvo_g[k, 2]
        total += lax.dot_general(
            jnp.concatenate([left, right], axis=1),
            jnp.concatenate([weight, weight], axis=0),
            NT,
            preferred_element_type=F32,
        )
    total += jnp.concatenate([bo_s[...], bo_s[...]], axis=1)
    o_g[s] = jnp.where(low, total[:16], total[16:]).astype(BF16)
    spread(o_g.at[s], o_g, 13)
    received(wu_g.at[pl.ds(0, 4)], 7)
    received(wd_g.at[pl.ds(0, 4)], 9)
    received(o_g.at[pl.ds(0, SEQ - 1)], 13)

    for j in range(HEADS):
        x_buf[:, 128 * j : 128 * j + 128] += unfold(o_g, j)
    n_buf[...] = layer_norm(x_buf[...], gain2_s[...], bias2_s[...]).astype(BF16)
    total = jnp.zeros((ROWS, 256), F32)
    for k in range(REQ):
        total += jnp.dot(n_buf[:, 256 * k : 256 * k + 256], wu_g[k], preferred_element_type=F32)
    total += bu_s[...]
    hidden = (0.5 * total * (1.0 + lax.erf(total * (0.5**0.5)))).astype(BF16)
    for k in range(REQ):
        feed = jnp.dot(hidden, wd_g[k], preferred_element_type=F32).astype(BF16)
        f_s[4 * k] = feed[:16, :128]
        f_s[4 * k + 1] = feed[16:, :128]
        f_s[4 * k + 2] = feed[:16, 128:]
        f_s[4 * k + 3] = feed[16:, 128:]

    def scatter(i, _):
        peer = far(i)
        send(f_s.at[peer], f_g.at[s], 14, (peer, r))
        return 0

    lax.fori_loop(0, SEQ - 1, scatter, 0)
    f_g[s] = f_s[s]
    columns = pl.ds(pl.multiple_of(head * 128, 128), 128)
    mid = x_buf[pl.ds(pl.multiple_of(half * 16, 16), 16), columns] + bd_s[:, columns]
    received(f_g.at[pl.ds(0, SEQ - 1)], 14)
    summed = f_g[0].astype(F32)
    for k in range(1, SEQ):
        summed += f_g[k].astype(F32)
    h_g[s] = (mid + summed).astype(BF16)
    spread(h_g.at[s], h_g, 15)

    store_keys.wait()
    store_values.wait()
    for buf, phase in ((wq_g, 0), (wkvo_g, 2), (wu_g, 6), (wd_g, 8)):
        sent(buf.at[pl.ds(0, 3)], phase)
        sent(buf.at[pl.ds(0, 4)], phase + 1)
    for buf, phase in ((q_g, 4), (kv_g, 5), (p_g, 10), (t_g, 11), (a_g, 12), (o_g, 13), (f_g, 14)):
        sent(buf.at[pl.ds(0, SEQ - 1)], phase)
    received(h_g.at[pl.ds(0, SEQ - 1)], 15)
    for j in range(HEADS):
        whole = jnp.concatenate([h_g[2 * j], h_g[2 * j + 1]], axis=0).astype(F32)
        for i in range(8):
            out[i, :, 128 * j : 128 * j + 128] = whole[4 * i : 4 * i + 4].astype(BF16)
    sent(h_g.at[pl.ds(0, SEQ - 1)], 15)


def finish(hidden, keys, values, out, out_keys, out_values, h_buf, k_buf, v_buf, in_sem, out_sem):
    half = SPOTS // 2
    moves = [(hidden, h_buf, out)]
    for a, b, c in ((keys, k_buf, out_keys), (values, v_buf, out_values)):
        for i in range(2):
            part = pl.ds(i * half, half)
            moves.append((a.at[part], b.at[part], c.at[part]))
    ins = [pltpu.make_async_copy(a, b, in_sem.at[i]) for i, (a, b, _) in enumerate(moves)]
    outs = [pltpu.make_async_copy(b, c, out_sem.at[i]) for i, (_, b, c) in enumerate(moves)]
    for copy in ins:
        copy.start()
    for arrived, copy in zip(ins, outs):
        arrived.wait()
        copy.start()
    for copy in outs:
        copy.wait()


def body(
    tokens,
    lengths,
    cache_keys,
    cache_values,
    norm1_gain,
    norm1_bias,
    w_query,
    b_query,
    w_key,
    b_key,
    w_value,
    b_value,
    w_out,
    b_out,
    norm2_gain,
    norm2_bias,
    w_up,
    b_up,
    w_down,
    b_down,
):
    vmem = pl.BlockSpec(memory_space=pltpu.VMEM)
    hbm = pl.BlockSpec(memory_space=pltpu.HBM)

    def line(v):
        return v.reshape(1, -1)

    slots = pltpu.VMEM((SEQ, 16, 128), BF16)
    hidden_out, new_keys, new_values = pl.pallas_call(
        kernel,
        out_shape=(
            jax.ShapeDtypeStruct((8, 4, WIDTH), BF16),
            jax.ShapeDtypeStruct((SPOTS, WIDTH), BF16),
            jax.ShapeDtypeStruct((SPOTS, WIDTH), BF16),
        ),
        in_specs=[hbm] * 20,
        out_specs=(vmem, hbm, hbm),
        scratch_shapes=[
            pltpu.VMEM((ROWS, WIDTH), F32),
            pltpu.VMEM((ROWS, WIDTH), BF16),
            pltpu.VMEM((SPOTS, WIDTH), BF16),
            pltpu.VMEM((SPOTS, WIDTH), BF16),
            pltpu.SMEM((8,), jnp.int32),
            pltpu.VMEM((8, 4, WIDTH), BF16),
            pltpu.VMEM((1, WIDTH), F32),
            pltpu.VMEM((1, WIDTH), F32),
            pltpu.VMEM((1, 64), F32),
            pltpu.VMEM((1, 64), F32),
            pltpu.VMEM((1, 64), F32),
            pltpu.VMEM((1, 64), F32),
            pltpu.VMEM((1, WIDTH), F32),
            pltpu.VMEM((1, WIDTH), F32),
            pltpu.VMEM((1, 256), F32),
            pltpu.VMEM((1, WIDTH), F32),
            pltpu.VMEM((REQ, 64, 256), BF16),
            pltpu.VMEM((REQ, 3, 64, 256), BF16),
            pltpu.VMEM((REQ, 256, 256), BF16),
            pltpu.VMEM((REQ, 256, 256), BF16),
            slots,
            pltpu.VMEM((SEQ, 2, 16, 128), BF16),
            slots,
            slots,
            pltpu.VMEM((HEADS, 1, 128), F32),
            pltpu.VMEM((SEQ, 1, 128), F32),
            slots,
            slots,
            slots,
            slots,
            slots,
            pltpu.SemaphoreType.DMA((20,)),
            pltpu.SemaphoreType.DMA((2,)),
            pltpu.SemaphoreType.DMA((16,)),
            pltpu.SemaphoreType.DMA((16,)),
        ],
        compiler_params=pltpu.CompilerParams(
            collective_id=0, has_side_effects=True, vmem_limit_bytes=58 * 1024 * 1024
        ),
        cost_estimate=pl.CostEstimate(flops=500_000_000, bytes_accessed=9_000_000, transcendentals=300_000),
    )(
        lengths,
        tokens,
        cache_keys.reshape(SPOTS, WIDTH),
        cache_values.reshape(SPOTS, WIDTH),
        line(norm1_gain),
        line(norm1_bias),
        w_query.T,
        line(b_query),
        w_key.T,
        line(b_key),
        w_value.T,
        line(b_value),
        w_out.T,
        line(b_out),
        line(norm2_gain),
        line(norm2_bias),
        w_up,
        line(b_up),
        w_down,
        line(b_down),
    )
    hidden_out, new_keys, new_values = pl.pallas_call(
        finish,
        out_shape=(
            jax.ShapeDtypeStruct((8, 4, WIDTH), BF16),
            jax.ShapeDtypeStruct((SPOTS, WIDTH), BF16),
            jax.ShapeDtypeStruct((SPOTS, WIDTH), BF16),
        ),
        in_specs=[hbm] * 3,
        out_specs=(hbm, hbm, hbm),
        scratch_shapes=[
            pltpu.VMEM((8, 4, WIDTH), BF16),
            pltpu.VMEM((SPOTS, WIDTH), BF16),
            pltpu.VMEM((SPOTS, WIDTH), BF16),
            pltpu.SemaphoreType.DMA((5,)),
            pltpu.SemaphoreType.DMA((5,)),
        ],
        compiler_params=pltpu.CompilerParams(vmem_limit_bytes=58 * 1024 * 1024),
    )(hidden_out, new_keys, new_values)
    return hidden_out, new_keys.reshape(8, 64, WIDTH), new_values.reshape(8, 64, WIDTH)


def solution(mesh):
    in_specs = (
        P("req", None, None),
        P("req"),
        P("req", "seq", None),
        P("req", "seq", None),
        P(),
        P(),
        P("req", "seq"),
        P("seq"),
        P("req", "seq"),
        P("seq"),
        P("req", "seq"),
        P("seq"),
        P("req", "seq"),
        P("seq"),
        P(),
        P(),
        P("req", "seq"),
        P("seq"),
        P("seq", "req"),
        P(),
    )
    out_specs = (P("req", None, None), P("req", "seq", None), P("req", "seq", None))
    return jax.shard_map(body, mesh=mesh, in_specs=in_specs, out_specs=out_specs, check_vma=False)
```

```python
import functools

import jax
import jax.numpy as jnp
from jax import lax
from jax.experimental import pallas as pl
from jax.experimental.pallas import tpu as pltpu
from jax.sharding import PartitionSpec as P

HEADS = 16
HEAD = 128
SEQ = 32
REQ = 8
ROWS = 32
WIDTH = 2048
SPOTS = 512
MESH = pl.DeviceIdType.MESH
F32 = jnp.float32
BF16 = jnp.bfloat16
NT = (((1,), (1,)), ((), ()))
ORDER = (
    ((0, 0), (0, 1), (1, 0), (7, 0)),
    ((1, 1), (7, 1), (2, 0), (6, 0)),
    ((4, 1), (4, 0), (3, 1), (5, 1)),
    ((3, 0), (5, 0), (2, 1), (6, 1)),
)


def layer_norm(values, gain, shift):
    center = values - jnp.mean(values, axis=-1, keepdims=True)
    spread = jnp.mean(center * center, axis=-1, keepdims=True)
    return center * lax.rsqrt(spread + 1e-05) * gain + shift


def far_first(i):
    a, b = i // 4, lax.rem(i, 4)
    dz = 4 + ((a + 1) // 2) * (1 - 2 * lax.rem(a, 2))
    dx = 2 + ((b + 1) // 2) * (1 - 2 * lax.rem(b, 2))
    return dz, dx


def unfold(slots, j):
    first = slots[2 * j].astype(F32)
    second = slots[2 * j + 1].astype(F32)
    low = lax.broadcasted_iota(jnp.int32, (16, 128), 1) < 64
    top = jnp.where(low, first, pltpu.roll(second, 64, 1))
    bottom = jnp.where(low, pltpu.roll(first, 64, 1), second)
    return jnp.concatenate([top, bottom], axis=0)


def kernel(
    lengths,
    tokens,
    cache_keys,
    cache_values,
    gain1,
    bias1,
    wq,
    bq,
    wk,
    bk,
    wv,
    bv,
    wo,
    bo,
    gain2,
    bias2,
    wu,
    bu,
    wd,
    bd,
    out,
    out_keys,
    out_values,
    x_buf,
    n_buf,
    k_buf,
    v_buf,
    lengths_s,
    tokens_s,
    gain1_s,
    bias1_s,
    bq_s,
    bk_s,
    bv_s,
    bo_s,
    gain2_s,
    bias2_s,
    bu_s,
    bd_s,
    wq_g,
    wkvo_g,
    wu_g,
    wd_g,
    q_g,
    kv_g,
    p_s,
    p_g,
    a_g,
    o_g,
    f_s,
    f_g,
    h_g,
    load_sem,
    store_sem,
    send_sem,
    recv_sem,
    query_sem,
    column_sem,
    plane_sem,
):
    s = lax.axis_index("seq")
    r = lax.axis_index("req")
    z, x = s // 4, lax.rem(s, 4)
    y, core = r // 2, lax.rem(r, 2)
    sibling = y * 2 + 1 - core
    head, half = s // 2, lax.rem(s, 2)
    partner = s + 1 - 2 * half

    barrier = pltpu.get_barrier_semaphore()

    def far(i):
        dz, dx = far_first(i)
        return lax.rem(z + dz, 8) * 4 + lax.rem(x + dx, 4)

    def along(dz, dx):
        return (lax.rem(z + dz, 8) * 4 + lax.rem(x + dx, 4), r)

    for dz, dx in ((2, 0), (6, 0), (0, 2), (1, 0), (7, 0), (0, 1), (0, 3)):
        pl.semaphore_signal(barrier, inc=1, device_id=along(dz, dx), device_id_type=MESH)
    for k in (4, 5, 2, 3, 6, 7, 1):
        near = lax.rem(y + k // 2, 4) * 2 + lax.rem(core + k, 2)
        pl.semaphore_signal(barrier, inc=1, device_id=(s, near), device_id_type=MESH)

    loads = [
        (tokens, tokens_s),
        (gain1, gain1_s),
        (bias1, bias1_s),
        (wq, wq_g.at[r]),
        (wk, wkvo_g.at[r, 0]),
        (wv, wkvo_g.at[r, 1]),
        (wo, wkvo_g.at[r, 2]),
        (bq, bq_s),
        (bk, bk_s),
        (bv, bv_s),
        (bo, bo_s),
        (lengths, lengths_s),
        (wu, wu_g.at[r]),
        (wd, wd_g.at[r]),
        (gain2, gain2_s),
        (bias2, bias2_s),
        (bu, bu_s),
        (bd, bd_s),
        (cache_keys, k_buf),
        (cache_values, v_buf),
    ]
    loads = [pltpu.make_async_copy(a, b, load_sem.at[i]) for i, (a, b) in enumerate(loads)]
    for load in loads:
        load.start()

    for load in loads[:3]:
        load.wait()
    for i in range(8):
        x_buf[4 * i : 4 * i + 4, :] = tokens_s[i].astype(F32)
    n_buf[...] = layer_norm(x_buf[...], gain1_s[...], bias1_s[...]).astype(BF16)

    def send(src, dst, phase, device):
        pltpu.make_async_remote_copy(
            src, dst, send_sem.at[phase], recv_sem.at[phase], device_id=device, device_id_type=MESH
        ).start()

    def received(ref, phase):
        pltpu.make_async_remote_copy(
            ref, ref, send_sem.at[phase], recv_sem.at[phase], device_id=(s, sibling), device_id_type=MESH
        ).wait_recv()

    def sent(ref, phase):
        pltpu.make_async_remote_copy(
            ref, ref, send_sem.at[phase], recv_sem.at[phase], device_id=(s, sibling), device_id_type=MESH
        ).wait_send()

    def spread(src, slots, phase):
        def one(i, _):
            send(src, slots.at[s], phase, (far(i), r))
            return 0

        lax.fori_loop(0, SEQ - 1, one, 0)

    def along_y(buf, phase):
        for k in (2, 1, 3):
            send(buf.at[r], buf.at[r], phase, (s, lax.rem(y + k, 4) * 2 + core))

    def across(buf, phase, own):
        for k in (0,) if own else (1, 3, 2):
            block = lax.rem(y + k, 4) * 2 + core
            send(buf.at[block], buf.at[block], phase, (s, sibling))

    for load in loads[3:12]:
        load.wait()
    pl.semaphore_wait(barrier, 14)
    for dz in (2, 6):
        pl.semaphore_signal(column_sem, inc=1, device_id=along(dz, 0), device_id_type=MESH)

    along_y(wq_g, 0)
    across(wq_g, 1, True)
    along_y(wkvo_g, 2)
    across(wkvo_g, 3, True)
    pl.semaphore_wait(column_sem, 2)
    for dx in (2, 1, 3):
        pl.semaphore_signal(plane_sem, inc=1, device_id=along(0, dx), device_id_type=MESH)
    received(wq_g.at[pl.ds(0, 3)], 0)
    across(wq_g, 1, False)
    received(wq_g.at[pl.ds(0, 4)], 1)

    low = lax.broadcasted_iota(jnp.int32, (16, 128), 1) < 64

    total = jnp.zeros((ROWS, 128), F32)
    for k in range(REQ):
        weight = wq_g[k]
        total += lax.dot_general(
            n_buf[:, 256 * k : 256 * k + 256],
            jnp.concatenate([weight, weight], axis=0),
            NT,
            preferred_element_type=F32,
        )
    total += jnp.concatenate([bq_s[...], bq_s[...]], axis=1)
    q_g[s] = jnp.where(low, total[:16], total[16:]).astype(BF16)

    pl.semaphore_wait(plane_sem, 3)

    def share_queries(i, _):
        pltpu.make_async_remote_copy(
            q_g.at[s],
            q_g.at[s],
            send_sem.at[4],
            query_sem.at[s],
            device_id=(far(i), r),
            device_id_type=MESH,
        ).start()
        return 0

    lax.fori_loop(0, SEQ - 1, share_queries, 0)

    received(wkvo_g.at[pl.ds(0, 3)], 2)
    across(wkvo_g, 3, False)
    for load in loads[12:]:
        load.wait()

    scale = HEAD**-0.5
    row = lax.broadcasted_iota(jnp.int32, (ROWS, SPOTS), 0)
    col = lax.broadcasted_iota(jnp.int32, (ROWS, SPOTS), 1)
    limit = jnp.zeros((ROWS, SPOTS), jnp.int32)
    for k in range(8):
        limit = jnp.where((row >> 2) == k, lengths_s[k], limit)
    valid = ((row >> 2) == (col >> 6)) & ((col & 63) + s * 64 < limit)
    lane = lax.broadcasted_iota(jnp.int32, (ROWS, 128), 1)
    marks = [lane == s + 32 * k for k in range(4)]

    def halves(value):
        first = value.astype(BF16).astype(F32)
        return first, (value - first).astype(BF16).astype(F32)

    for group in ORDER:
        heads = [(lax.rem(z + dz, 8) * 2 + lax.rem(x // 2 + dp, 2), dz + dp == 0) for dz, dp in group]
        for j, own in heads:
            for peer in (partner,) if own else (2 * j, 2 * j + 1):
                pltpu.make_async_copy(q_g.at[peer], q_g.at[peer], query_sem.at[peer]).wait()
        columns = [pl.ds(pl.multiple_of(j * 128, 128), 128) for j, _ in heads]
        scores = [
            lax.dot_general(
                unfold(q_g, j).astype(BF16), k_buf[:, columns[k]], NT, preferred_element_type=F32
            )
            for k, (j, _) in enumerate(heads)
        ]
        scores = [jnp.where(valid, score * scale, -1e30) for score in scores]
        peaks = [halves(jnp.maximum(jnp.max(score, axis=1, keepdims=True), -1e20)) for score in scores]
        expos = [jnp.exp(score - (peak[0] + peak[1])) for score, peak in zip(scores, peaks)]
        amounts = [halves(jnp.sum(expo, axis=1, keepdims=True)) for expo in expos]
        parts = [
            jnp.dot(expo.astype(BF16), v_buf[:, column], preferred_element_type=F32).astype(BF16)
            for expo, column in zip(expos, columns)
        ]
        for k, (j, own) in enumerate(heads):
            stats = jnp.zeros((ROWS, 128), F32)
            for mark, value in zip(marks, peaks[k] + amounts[k]):
                stats = jnp.where(mark, value, stats)
            stats = stats.astype(BF16)
            p_s[2 * j, 0:16] = parts[k][:16]
            p_s[2 * j, 16:32] = stats[:16]
            p_s[2 * j + 1, 0:16] = parts[k][16:]
            p_s[2 * j + 1, 16:32] = stats[16:]
            for peer in (partner,) if own else (2 * j, 2 * j + 1):
                send(p_s.at[peer], p_g.at[s], 10, (peer, r))
    p_g[s] = p_s[s]

    received(wkvo_g.at[pl.ds(0, 4)], 3)
    total = jnp.zeros((ROWS, 128), F32)
    for k in range(REQ):
        total += lax.dot_general(
            n_buf[:, 256 * k : 256 * k + 256],
            wkvo_g[k, 0:2].reshape(128, 256),
            NT,
            preferred_element_type=F32,
        )
    total += jnp.concatenate([bk_s[...], bv_s[...]], axis=1)
    kv_g[s, 0] = jnp.where(low, total[:16], pltpu.roll(total[16:], 64, 1)).astype(BF16)
    kv_g[s, 1] = jnp.where(low, pltpu.roll(total[:16], 64, 1), total[16:]).astype(BF16)
    send(kv_g.at[s], kv_g.at[s], 11, (partner, r))

    def share_rows(i, _):
        peer = far(i)

        @pl.when(peer != partner)
        def _():
            send(kv_g.at[s], kv_g.at[s], 5, (peer, r))

        return 0

    lax.fori_loop(0, SEQ - 1, share_rows, 0)

    along_y(wu_g, 6)
    across(wu_g, 7, True)
    along_y(wd_g, 8)
    across(wd_g, 9, True)

    def mine(slots):
        return unfold(slots, head)

    received(kv_g.at[0], 11)
    query = mine(q_g)
    query = jnp.where(half == 0, query[:16], query[16:]).astype(BF16)
    fresh_keys = mine(kv_g.at[:, 0]).astype(BF16)
    fresh_values = mine(kv_g.at[:, 1]).astype(BF16)
    row = lax.broadcasted_iota(jnp.int32, (16, ROWS), 0) + half * 16
    col = lax.broadcasted_iota(jnp.int32, (16, ROWS), 1)
    scores = lax.dot_general(query, fresh_keys, NT, preferred_element_type=F32) * scale
    scores = jnp.where(((row >> 2) == (col >> 2)) & ((col & 3) <= (row & 3)), scores, -1e30)
    peak_new = jnp.max(scores, axis=1, keepdims=True)
    expo = jnp.exp(scores - peak_new)
    total_new = jnp.sum(expo, axis=1, keepdims=True)
    part_new = jnp.dot(expo.astype(BF16), fresh_values, preferred_element_type=F32)

    received(p_g.at[pl.ds(0, SEQ - 1)], 10)
    stats = p_g[0, 16:32].astype(F32)
    for k in range(1, SEQ):
        stats += p_g[k, 16:32].astype(F32)
    stats += pltpu.roll(stats, 96, 1)
    lane = lax.broadcasted_iota(jnp.int32, (16, 128), 1)
    peaks = jnp.where(lane < 32, stats, -1e20)
    totals = jnp.where(lane < 32, pltpu.roll(stats, 64, 1), 0.0)
    peak = jnp.maximum(jnp.max(peaks, axis=1, keepdims=True), peak_new)
    share_new = jnp.exp(peak_new - peak)
    shares = jnp.exp(peaks - peak)
    total = jnp.sum(shares * totals, axis=1, keepdims=True) + share_new * total_new
    mixed = share_new * part_new
    for k in range(SEQ):
        mixed += shares[:, k : k + 1] * p_g[k, 0:16].astype(F32)
    a_g[s] = (mixed / total).astype(BF16)
    spread(a_g.at[s], a_g, 12)

    received(kv_g.at[pl.ds(0, SEQ - 2)], 5)
    spot = lax.broadcasted_iota(jnp.int32, (SPOTS, ROWS), 0)
    new = lax.broadcasted_iota(jnp.int32, (SPOTS, ROWS), 1)
    start = jnp.zeros((SPOTS, ROWS), jnp.int32)
    for k in range(8):
        start = jnp.where((new >> 2) == k, lengths_s[k], start)
    hit = ((new >> 2) == (spot >> 6)) & ((spot & 63) + s * 64 == start + (new & 3))
    pick = jnp.where(hit, 1.0, 0.0)
    changed = jnp.max(pick, axis=1, keepdims=True) > 0.5
    pick = pick.astype(BF16)

    def renew(which, buf):
        def four(g, _):
            columns = [pl.ds(pl.multiple_of((4 * g + j) * 128, 128), 128) for j in range(4)]
            rows = [unfold(kv_g.at[:, which], 4 * g + j).astype(BF16) for j in range(4)]
            fresh = [jnp.dot(pick, row, preferred_element_type=F32) for row in rows]
            for j in range(4):
                old = buf[:, columns[j]].astype(F32)
                buf[:, columns[j]] = jnp.where(changed, fresh[j], old).astype(BF16)
            return 0

        lax.fori_loop(0, HEADS // 4, four, 0)

    renew(0, k_buf)
    store_keys = pltpu.make_async_copy(k_buf, out_keys, store_sem.at[0])
    store_keys.start()

    received(wu_g.at[pl.ds(0, 3)], 6)
    across(wu_g, 7, False)
    received(wd_g.at[pl.ds(0, 3)], 8)
    across(wd_g, 9, False)
    received(a_g.at[pl.ds(0, SEQ - 1)], 12)
    total = jnp.zeros((ROWS, 128), F32)
    for k in range(REQ):
        left = jnp.concatenate([a_g[4 * k], a_g[4 * k + 1]], axis=0)
        right = jnp.concatenate([a_g[4 * k + 2], a_g[4 * k + 3]], axis=0)
        weight = wkvo_g[k, 2]
        total += lax.dot_general(
            jnp.concatenate([left, right], axis=1),
            jnp.concatenate([weight, weight], axis=0),
            NT,
            preferred_element_type=F32,
        )
    total += jnp.concatenate([bo_s[...], bo_s[...]], axis=1)
    o_g[s] = jnp.where(low, total[:16], total[16:]).astype(BF16)
    spread(o_g.at[s], o_g, 13)
    renew(1, v_buf)
    store_values = pltpu.make_async_copy(v_buf, out_values, store_sem.at[1])
    store_values.start()
    received(wu_g.at[pl.ds(0, 4)], 7)
    received(wd_g.at[pl.ds(0, 4)], 9)
    received(o_g.at[pl.ds(0, SEQ - 1)], 13)

    for j in range(HEADS):
        x_buf[:, 128 * j : 128 * j + 128] += unfold(o_g, j)
    n_buf[...] = layer_norm(x_buf[...], gain2_s[...], bias2_s[...]).astype(BF16)
    total = jnp.zeros((ROWS, 256), F32)
    for k in range(REQ):
        total += jnp.dot(n_buf[:, 256 * k : 256 * k + 256], wu_g[k], preferred_element_type=F32)
    total += bu_s[...]
    hidden = (0.5 * total * (1.0 + lax.erf(total * (0.5**0.5)))).astype(BF16)
    for k in range(REQ):
        feed = jnp.dot(hidden, wd_g[k], preferred_element_type=F32).astype(BF16)
        f_s[4 * k] = feed[:16, :128]
        f_s[4 * k + 1] = feed[16:, :128]
        f_s[4 * k + 2] = feed[:16, 128:]
        f_s[4 * k + 3] = feed[16:, 128:]

    def scatter(i, _):
        peer = far(i)
        send(f_s.at[peer], f_g.at[s], 14, (peer, r))
        return 0

    lax.fori_loop(0, SEQ - 1, scatter, 0)
    f_g[s] = f_s[s]
    columns = pl.ds(pl.multiple_of(head * 128, 128), 128)
    mid = x_buf[pl.ds(pl.multiple_of(half * 16, 16), 16), columns] + bd_s[:, columns]
    received(f_g.at[pl.ds(0, SEQ - 1)], 14)
    summed = f_g[0].astype(F32)
    for k in range(1, SEQ):
        summed += f_g[k].astype(F32)
    h_g[s] = (mid + summed).astype(BF16)
    spread(h_g.at[s], h_g, 15)

    store_keys.wait()
    store_values.wait()
    for buf, phase in ((wq_g, 0), (wkvo_g, 2), (wu_g, 6), (wd_g, 8)):
        sent(buf.at[pl.ds(0, 3)], phase)
        sent(buf.at[pl.ds(0, 4)], phase + 1)
    for buf, phase in ((q_g, 4), (p_g, 10), (a_g, 12), (o_g, 13), (f_g, 14)):
        sent(buf.at[pl.ds(0, SEQ - 1)], phase)
    sent(kv_g.at[pl.ds(0, SEQ - 2)], 5)
    sent(kv_g.at[0], 11)
    received(h_g.at[pl.ds(0, SEQ - 1)], 15)
    for j in range(HEADS):
        whole = jnp.concatenate([h_g[2 * j], h_g[2 * j + 1]], axis=0).astype(F32)
        for i in range(8):
            out[i, :, 128 * j : 128 * j + 128] = whole[4 * i : 4 * i + 4].astype(BF16)
    sent(h_g.at[pl.ds(0, SEQ - 1)], 15)


def finish(hidden, keys, values, out, out_keys, out_values, h_buf, k_buf, v_buf, in_sem, out_sem):
    half = SPOTS // 2
    moves = [(hidden, h_buf, out)]
    for a, b, c in ((keys, k_buf, out_keys), (values, v_buf, out_values)):
        for i in range(2):
            part = pl.ds(i * half, half)
            moves.append((a.at[part], b.at[part], c.at[part]))
    ins = [pltpu.make_async_copy(a, b, in_sem.at[i]) for i, (a, b, _) in enumerate(moves)]
    outs = [pltpu.make_async_copy(b, c, out_sem.at[i]) for i, (_, b, c) in enumerate(moves)]
    for copy in ins:
        copy.start()
    for arrived, copy in zip(ins, outs):
        arrived.wait()
        copy.start()
    for copy in outs:
        copy.wait()


def body(
    tokens,
    lengths,
    cache_keys,
    cache_values,
    norm1_gain,
    norm1_bias,
    w_query,
    b_query,
    w_key,
    b_key,
    w_value,
    b_value,
    w_out,
    b_out,
    norm2_gain,
    norm2_bias,
    w_up,
    b_up,
    w_down,
    b_down,
):
    vmem = pl.BlockSpec(memory_space=pltpu.VMEM)
    hbm = pl.BlockSpec(memory_space=pltpu.HBM)

    def line(v):
        return v.reshape(1, -1)

    slots = pltpu.VMEM((SEQ, 16, 128), BF16)
    hidden_out, new_keys, new_values = pl.pallas_call(
        kernel,
        out_shape=(
            jax.ShapeDtypeStruct((8, 4, WIDTH), BF16),
            jax.ShapeDtypeStruct((SPOTS, WIDTH), BF16),
            jax.ShapeDtypeStruct((SPOTS, WIDTH), BF16),
        ),
        in_specs=[hbm] * 20,
        out_specs=(vmem, hbm, hbm),
        scratch_shapes=[
            pltpu.VMEM((ROWS, WIDTH), F32),
            pltpu.VMEM((ROWS, WIDTH), BF16),
            pltpu.VMEM((SPOTS, WIDTH), BF16),
            pltpu.VMEM((SPOTS, WIDTH), BF16),
            pltpu.SMEM((8,), jnp.int32),
            pltpu.VMEM((8, 4, WIDTH), BF16),
            pltpu.VMEM((1, WIDTH), F32),
            pltpu.VMEM((1, WIDTH), F32),
            pltpu.VMEM((1, 64), F32),
            pltpu.VMEM((1, 64), F32),
            pltpu.VMEM((1, 64), F32),
            pltpu.VMEM((1, 64), F32),
            pltpu.VMEM((1, WIDTH), F32),
            pltpu.VMEM((1, WIDTH), F32),
            pltpu.VMEM((1, 256), F32),
            pltpu.VMEM((1, WIDTH), F32),
            pltpu.VMEM((REQ, 64, 256), BF16),
            pltpu.VMEM((REQ, 3, 64, 256), BF16),
            pltpu.VMEM((REQ, 256, 256), BF16),
            pltpu.VMEM((REQ, 256, 256), BF16),
            slots,
            pltpu.VMEM((SEQ, 2, 16, 128), BF16),
            pltpu.VMEM((SEQ, 32, 128), BF16),
            pltpu.VMEM((SEQ, 32, 128), BF16),
            slots,
            slots,
            slots,
            slots,
            slots,
            pltpu.SemaphoreType.DMA((20,)),
            pltpu.SemaphoreType.DMA((2,)),
            pltpu.SemaphoreType.DMA((16,)),
            pltpu.SemaphoreType.DMA((16,)),
            pltpu.SemaphoreType.DMA((SEQ,)),
            pltpu.SemaphoreType.REGULAR,
            pltpu.SemaphoreType.REGULAR,
        ],
        compiler_params=pltpu.CompilerParams(
            collective_id=0, has_side_effects=True, vmem_limit_bytes=58 * 1024 * 1024
        ),
        cost_estimate=pl.CostEstimate(flops=500_000_000, bytes_accessed=9_000_000, transcendentals=300_000),
    )(
        lengths,
        tokens,
        cache_keys.reshape(SPOTS, WIDTH),
        cache_values.reshape(SPOTS, WIDTH),
        line(norm1_gain),
        line(norm1_bias),
        w_query.T,
        line(b_query),
        w_key.T,
        line(b_key),
        w_value.T,
        line(b_value),
        w_out.T,
        line(b_out),
        line(norm2_gain),
        line(norm2_bias),
        w_up,
        line(b_up),
        w_down,
        line(b_down),
    )
    hidden_out, new_keys, new_values = pl.pallas_call(
        finish,
        out_shape=(
            jax.ShapeDtypeStruct((8, 4, WIDTH), BF16),
            jax.ShapeDtypeStruct((SPOTS, WIDTH), BF16),
            jax.ShapeDtypeStruct((SPOTS, WIDTH), BF16),
        ),
        in_specs=[hbm] * 3,
        out_specs=(hbm, hbm, hbm),
        scratch_shapes=[
            pltpu.VMEM((8, 4, WIDTH), BF16),
            pltpu.VMEM((SPOTS, WIDTH), BF16),
            pltpu.VMEM((SPOTS, WIDTH), BF16),
            pltpu.SemaphoreType.DMA((5,)),
            pltpu.SemaphoreType.DMA((5,)),
        ],
        compiler_params=pltpu.CompilerParams(vmem_limit_bytes=58 * 1024 * 1024),
    )(hidden_out, new_keys, new_values)
    return hidden_out, new_keys.reshape(8, 64, WIDTH), new_values.reshape(8, 64, WIDTH)


def solution(mesh):
    in_specs = (
        P("req", None, None),
        P("req"),
        P("req", "seq", None),
        P("req", "seq", None),
        P(),
        P(),
        P("req", "seq"),
        P("seq"),
        P("req", "seq"),
        P("seq"),
        P("req", "seq"),
        P("seq"),
        P("req", "seq"),
        P("seq"),
        P(),
        P(),
        P("req", "seq"),
        P("seq"),
        P("seq", "req"),
        P(),
    )
    out_specs = (P("req", None, None), P("req", "seq", None), P("req", "seq", None))
    return jax.shard_map(body, mesh=mesh, in_specs=in_specs, out_specs=out_specs, check_vma=False)
```

```python
import functools

import jax
import jax.numpy as jnp
from jax import lax
from jax.experimental import pallas as pl
from jax.experimental.pallas import tpu as pltpu
from jax.sharding import PartitionSpec as P

HEADS = 16
HEAD = 128
SEQ = 32
REQ = 8
ROWS = 32
WIDTH = 2048
SPOTS = 512
MESH = pl.DeviceIdType.MESH
F32 = jnp.float32
BF16 = jnp.bfloat16
NT = (((1,), (1,)), ((), ()))
ORDER = (
    ((0, 0), (0, 1), (1, 0), (7, 0)),
    ((1, 1), (7, 1), (2, 0), (6, 0)),
    ((4, 1), (4, 0), (3, 1), (5, 1)),
    ((3, 0), (5, 0), (2, 1), (6, 1)),
)


def layer_norm(values, gain, shift):
    center = values - jnp.mean(values, axis=-1, keepdims=True)
    spread = jnp.mean(center * center, axis=-1, keepdims=True)
    return center * lax.rsqrt(spread + 1e-05) * gain + shift


def far_first(i):
    a, b = i // 4, lax.rem(i, 4)
    dz = 4 + ((a + 1) // 2) * (1 - 2 * lax.rem(a, 2))
    dx = 2 + ((b + 1) // 2) * (1 - 2 * lax.rem(b, 2))
    return dz, dx


def unfold(slots, j):
    return unfold_pair(slots[2 * j], slots[2 * j + 1])


def unfold_pair(first, second):
    first, second = first.astype(F32), second.astype(F32)
    low = lax.broadcasted_iota(jnp.int32, (16, 128), 1) < 64
    top = jnp.where(low, first, pltpu.roll(second, 64, 1))
    bottom = jnp.where(low, pltpu.roll(first, 64, 1), second)
    return jnp.concatenate([top, bottom], axis=0)


def kernel(
    lengths,
    tokens,
    cache_keys,
    cache_values,
    gain1,
    bias1,
    wq,
    bq,
    wk,
    bk,
    wv,
    bv,
    wo,
    bo,
    gain2,
    bias2,
    wu,
    bu,
    wd,
    bd,
    out,
    out_keys,
    out_values,
    x_buf,
    n_buf,
    k_buf,
    v_buf,
    lengths_s,
    tokens_s,
    gain1_s,
    bias1_s,
    bq_s,
    bk_s,
    bv_s,
    bo_s,
    gain2_s,
    bias2_s,
    bu_s,
    bd_s,
    wq_g,
    wkvo_g,
    wu_g,
    wd_g,
    q_g,
    kv_g,
    kv_p,
    p_s,
    p_g,
    a_g,
    o_g,
    f_s,
    f_g,
    h_g,
    load_sem,
    store_sem,
    send_sem,
    recv_sem,
    query_sem,
    column_sem,
    plane_sem,
):
    s = lax.axis_index("seq")
    r = lax.axis_index("req")
    z, x = s // 4, lax.rem(s, 4)
    y, core = r // 2, lax.rem(r, 2)
    sibling = y * 2 + 1 - core
    head, half = s // 2, lax.rem(s, 2)
    partner = s + 1 - 2 * half

    barrier = pltpu.get_barrier_semaphore()

    def far(i):
        dz, dx = far_first(i)
        return lax.rem(z + dz, 8) * 4 + lax.rem(x + dx, 4)

    def along(dz, dx):
        return (lax.rem(z + dz, 8) * 4 + lax.rem(x + dx, 4), r)

    for dz, dx in ((2, 0), (6, 0), (0, 2), (1, 0), (7, 0), (0, 1), (0, 3)):
        pl.semaphore_signal(barrier, inc=1, device_id=along(dz, dx), device_id_type=MESH)
    for k in (4, 5, 2, 3, 6, 7, 1):
        near = lax.rem(y + k // 2, 4) * 2 + lax.rem(core + k, 2)
        pl.semaphore_signal(barrier, inc=1, device_id=(s, near), device_id_type=MESH)

    loads = [
        (tokens, tokens_s),
        (gain1, gain1_s),
        (bias1, bias1_s),
        (wq, wq_g.at[r]),
        (wk, wkvo_g.at[r, 0]),
        (wv, wkvo_g.at[r, 1]),
        (wo, wkvo_g.at[r, 2]),
        (bq, bq_s),
        (bk, bk_s),
        (bv, bv_s),
        (bo, bo_s),
        (lengths, lengths_s),
        (wu, wu_g.at[r]),
        (wd, wd_g.at[r]),
        (gain2, gain2_s),
        (bias2, bias2_s),
        (bu, bu_s),
        (bd, bd_s),
        (cache_keys, k_buf),
        (cache_values, v_buf),
    ]
    loads = [pltpu.make_async_copy(a, b, load_sem.at[i]) for i, (a, b) in enumerate(loads)]
    for load in loads:
        load.start()

    for load in loads[:3]:
        load.wait()
    for i in range(8):
        x_buf[4 * i : 4 * i + 4, :] = tokens_s[i].astype(F32)
    n_buf[...] = layer_norm(x_buf[...], gain1_s[...], bias1_s[...]).astype(BF16)

    def send(src, dst, phase, device):
        pltpu.make_async_remote_copy(
            src, dst, send_sem.at[phase], recv_sem.at[phase], device_id=device, device_id_type=MESH
        ).start()

    def received(ref, phase):
        pltpu.make_async_remote_copy(
            ref, ref, send_sem.at[phase], recv_sem.at[phase], device_id=(s, sibling), device_id_type=MESH
        ).wait_recv()

    def sent(ref, phase):
        pltpu.make_async_remote_copy(
            ref, ref, send_sem.at[phase], recv_sem.at[phase], device_id=(s, sibling), device_id_type=MESH
        ).wait_send()

    def spread(src, slots, phase):
        def one(i, _):
            send(src, slots.at[s], phase, (far(i), r))
            return 0

        lax.fori_loop(0, SEQ - 1, one, 0)

    def along_y(buf, phase):
        for k in (2, 1, 3):
            send(buf.at[r], buf.at[r], phase, (s, lax.rem(y + k, 4) * 2 + core))

    def across(buf, phase, own):
        for k in (0,) if own else (1, 3, 2):
            block = lax.rem(y + k, 4) * 2 + core
            send(buf.at[block], buf.at[block], phase, (s, sibling))

    for load in loads[3:12]:
        load.wait()
    pl.semaphore_wait(barrier, 14)
    for dz in (2, 6):
        pl.semaphore_signal(column_sem, inc=1, device_id=along(dz, 0), device_id_type=MESH)

    along_y(wq_g, 0)
    across(wq_g, 1, True)
    along_y(wkvo_g, 2)
    across(wkvo_g, 3, True)
    pl.semaphore_wait(column_sem, 2)
    for dx in (2, 1, 3):
        pl.semaphore_signal(plane_sem, inc=1, device_id=along(0, dx), device_id_type=MESH)
    received(wq_g.at[pl.ds(0, 3)], 0)
    across(wq_g, 1, False)
    received(wq_g.at[pl.ds(0, 4)], 1)

    low = lax.broadcasted_iota(jnp.int32, (16, 128), 1) < 64

    total = jnp.zeros((ROWS, 128), F32)
    for k in range(REQ):
        weight = wq_g[k]
        total += lax.dot_general(
            n_buf[:, 256 * k : 256 * k + 256],
            jnp.concatenate([weight, weight], axis=0),
            NT,
            preferred_element_type=F32,
        )
    total += jnp.concatenate([bq_s[...], bq_s[...]], axis=1)
    q_g[s] = jnp.where(low, total[:16], total[16:]).astype(BF16)

    pl.semaphore_wait(plane_sem, 3)

    def share_queries(i, _):
        pltpu.make_async_remote_copy(
            q_g.at[s],
            q_g.at[s],
            send_sem.at[4],
            query_sem.at[s],
            device_id=(far(i), r),
            device_id_type=MESH,
        ).start()
        return 0

    lax.fori_loop(0, SEQ - 1, share_queries, 0)

    received(wkvo_g.at[pl.ds(0, 3)], 2)
    across(wkvo_g, 3, False)
    for load in loads[12:]:
        load.wait()

    along_y(wu_g, 6)
    across(wu_g, 7, True)
    along_y(wd_g, 8)
    across(wd_g, 9, True)

    scale = HEAD**-0.5
    row = lax.broadcasted_iota(jnp.int32, (ROWS, SPOTS), 0)
    col = lax.broadcasted_iota(jnp.int32, (ROWS, SPOTS), 1)
    limit = jnp.zeros((ROWS, SPOTS), jnp.int32)
    for k in range(8):
        limit = jnp.where((row >> 2) == k, lengths_s[k], limit)
    valid = ((row >> 2) == (col >> 6)) & ((col & 63) + s * 64 < limit)
    lane = lax.broadcasted_iota(jnp.int32, (ROWS, 128), 1)
    marks = [lane == s + 32 * k for k in range(4)]

    def halves(value):
        first = value.astype(BF16).astype(F32)
        return first, (value - first).astype(BF16).astype(F32)

    for group in ORDER:
        heads = [(lax.rem(z + dz, 8) * 2 + lax.rem(x // 2 + dp, 2), dz + dp == 0) for dz, dp in group]
        for j, own in heads:
            for peer in (partner,) if own else (2 * j, 2 * j + 1):
                pltpu.make_async_copy(q_g.at[peer], q_g.at[peer], query_sem.at[peer]).wait()
        columns = [pl.ds(pl.multiple_of(j * 128, 128), 128) for j, _ in heads]
        scores = [
            lax.dot_general(
                unfold(q_g, j).astype(BF16), k_buf[:, columns[k]], NT, preferred_element_type=F32
            )
            for k, (j, _) in enumerate(heads)
        ]
        scores = [jnp.where(valid, score * scale, -1e30) for score in scores]
        peaks = [halves(jnp.maximum(jnp.max(score, axis=1, keepdims=True), -1e20)) for score in scores]
        expos = [jnp.exp(score - (peak[0] + peak[1])) for score, peak in zip(scores, peaks)]
        amounts = [halves(jnp.sum(expo, axis=1, keepdims=True)) for expo in expos]
        parts = [
            jnp.dot(expo.astype(BF16), v_buf[:, column], preferred_element_type=F32).astype(BF16)
            for expo, column in zip(expos, columns)
        ]
        for k, (j, own) in enumerate(heads):
            stats = jnp.zeros((ROWS, 128), F32)
            for mark, value in zip(marks, peaks[k] + amounts[k]):
                stats = jnp.where(mark, value, stats)
            stats = stats.astype(BF16)
            p_s[2 * j, 0:16] = parts[k][:16]
            p_s[2 * j, 16:32] = stats[:16]
            p_s[2 * j + 1, 0:16] = parts[k][16:]
            p_s[2 * j + 1, 16:32] = stats[16:]
            for peer in (partner,) if own else (2 * j, 2 * j + 1):
                send(p_s.at[peer], p_g.at[s], 10, (peer, r))
    p_g[s] = p_s[s]

    received(wkvo_g.at[pl.ds(0, 4)], 3)
    total = jnp.zeros((ROWS, 128), F32)
    for k in range(REQ):
        total += lax.dot_general(
            n_buf[:, 256 * k : 256 * k + 256],
            wkvo_g[k, 0:2].reshape(128, 256),
            NT,
            preferred_element_type=F32,
        )
    total += jnp.concatenate([bk_s[...], bv_s[...]], axis=1)
    kv_g[x, z, 0] = jnp.where(low, total[:16], pltpu.roll(total[16:], 64, 1)).astype(BF16)
    kv_g[x, z, 1] = jnp.where(low, pltpu.roll(total[:16], 64, 1), total[16:]).astype(BF16)
    send(kv_g.at[x, z], kv_p, 11, (partner, r))

    def mine(which):
        own, other = kv_g[x, z, which].astype(F32), kv_p[which].astype(F32)
        first, second = jnp.where(half == 0, own, other), jnp.where(half == 0, other, own)
        return unfold_pair(first, second).astype(BF16)

    received(kv_p, 11)
    query = unfold(q_g, head)
    query = jnp.where(half == 0, query[:16], query[16:]).astype(BF16)
    fresh_keys = mine(0)
    fresh_values = mine(1)
    row = lax.broadcasted_iota(jnp.int32, (16, ROWS), 0) + half * 16
    col = lax.broadcasted_iota(jnp.int32, (16, ROWS), 1)
    scores = lax.dot_general(query, fresh_keys, NT, preferred_element_type=F32) * scale
    scores = jnp.where(((row >> 2) == (col >> 2)) & ((col & 3) <= (row & 3)), scores, -1e30)
    peak_new = jnp.max(scores, axis=1, keepdims=True)
    expo = jnp.exp(scores - peak_new)
    total_new = jnp.sum(expo, axis=1, keepdims=True)
    part_new = jnp.dot(expo.astype(BF16), fresh_values, preferred_element_type=F32)

    received(p_g.at[pl.ds(0, SEQ - 1)], 10)
    stats = p_g[0, 16:32].astype(F32)
    for k in range(1, SEQ):
        stats += p_g[k, 16:32].astype(F32)
    stats += pltpu.roll(stats, 96, 1)
    lane = lax.broadcasted_iota(jnp.int32, (16, 128), 1)
    peaks = jnp.where(lane < 32, stats, -1e20)
    totals = jnp.where(lane < 32, pltpu.roll(stats, 64, 1), 0.0)
    peak = jnp.maximum(jnp.max(peaks, axis=1, keepdims=True), peak_new)
    share_new = jnp.exp(peak_new - peak)
    shares = jnp.exp(peaks - peak)
    total = jnp.sum(shares * totals, axis=1, keepdims=True) + share_new * total_new
    mixed = share_new * part_new
    for k in range(SEQ):
        mixed += shares[:, k : k + 1] * p_g[k, 0:16].astype(F32)
    a_g[s] = (mixed / total).astype(BF16)
    spread(a_g.at[s], a_g, 12)

    for dz in (4, 3, 5, 2, 6, 1, 7):
        send(kv_g.at[x, z], kv_g.at[x, z], 5, along(dz, 0))

    received(wu_g.at[pl.ds(0, 3)], 6)
    across(wu_g, 7, False)
    received(wd_g.at[pl.ds(0, 3)], 8)
    across(wd_g, 9, False)
    received(a_g.at[pl.ds(0, SEQ - 1)], 12)
    total = jnp.zeros((ROWS, 128), F32)
    for k in range(REQ):
        left = jnp.concatenate([a_g[4 * k], a_g[4 * k + 1]], axis=0)
        right = jnp.concatenate([a_g[4 * k + 2], a_g[4 * k + 3]], axis=0)
        weight = wkvo_g[k, 2]
        total += lax.dot_general(
            jnp.concatenate([left, right], axis=1),
            jnp.concatenate([weight, weight], axis=0),
            NT,
            preferred_element_type=F32,
        )
    total += jnp.concatenate([bo_s[...], bo_s[...]], axis=1)
    o_g[s] = jnp.where(low, total[:16], total[16:]).astype(BF16)
    spread(o_g.at[s], o_g, 13)
    received(kv_g.at[0, pl.ds(0, 7)], 5)
    for dx in (2, 1, 3):
        send(kv_g.at[x], kv_g.at[x], 16, along(0, dx))

    received(wu_g.at[pl.ds(0, 4)], 7)
    received(wd_g.at[pl.ds(0, 4)], 9)
    received(o_g.at[pl.ds(0, SEQ - 1)], 13)

    for j in range(HEADS):
        x_buf[:, 128 * j : 128 * j + 128] += unfold(o_g, j)
    n_buf[...] = layer_norm(x_buf[...], gain2_s[...], bias2_s[...]).astype(BF16)
    total = jnp.zeros((ROWS, 256), F32)
    for k in range(REQ):
        total += jnp.dot(n_buf[:, 256 * k : 256 * k + 256], wu_g[k], preferred_element_type=F32)
    total += bu_s[...]
    hidden = (0.5 * total * (1.0 + lax.erf(total * (0.5**0.5)))).astype(BF16)
    for k in range(REQ):
        feed = jnp.dot(hidden, wd_g[k], preferred_element_type=F32).astype(BF16)
        f_s[4 * k] = feed[:16, :128]
        f_s[4 * k + 1] = feed[16:, :128]
        f_s[4 * k + 2] = feed[:16, 128:]
        f_s[4 * k + 3] = feed[16:, 128:]

    def scatter(i, _):
        peer = far(i)
        send(f_s.at[peer], f_g.at[s], 14, (peer, r))
        return 0

    lax.fori_loop(0, SEQ - 1, scatter, 0)
    f_g[s] = f_s[s]

    received(kv_g.at[pl.ds(0, 3)], 16)
    spot = lax.broadcasted_iota(jnp.int32, (SPOTS, ROWS), 0)
    new = lax.broadcasted_iota(jnp.int32, (SPOTS, ROWS), 1)
    start = jnp.zeros((SPOTS, ROWS), jnp.int32)
    for k in range(8):
        start = jnp.where((new >> 2) == k, lengths_s[k], start)
    hit = ((new >> 2) == (spot >> 6)) & ((spot & 63) + s * 64 == start + (new & 3))
    pick = jnp.where(hit, 1.0, 0.0)
    changed = jnp.max(pick, axis=1, keepdims=True) > 0.5
    pick = pick.astype(BF16)

    def renew(which, buf):
        def four(g, _):
            columns = [pl.ds(pl.multiple_of((4 * g + j) * 128, 128), 128) for j in range(4)]
            rows = [
                unfold_pair(
                    kv_g[2 * (j % 2), 2 * g + j // 2, which], kv_g[2 * (j % 2) + 1, 2 * g + j // 2, which]
                ).astype(BF16)
                for j in range(4)
            ]
            fresh = [jnp.dot(pick, row, preferred_element_type=F32) for row in rows]
            for j in range(4):
                old = buf[:, columns[j]].astype(F32)
                buf[:, columns[j]] = jnp.where(changed, fresh[j], old).astype(BF16)
            return 0

        lax.fori_loop(0, HEADS // 4, four, 0)

    renew(0, k_buf)
    store_keys = pltpu.make_async_copy(k_buf, out_keys, store_sem.at[0])
    store_keys.start()

    columns = pl.ds(pl.multiple_of(head * 128, 128), 128)
    mid = x_buf[pl.ds(pl.multiple_of(half * 16, 16), 16), columns] + bd_s[:, columns]
    received(f_g.at[pl.ds(0, SEQ - 1)], 14)
    summed = f_g[0].astype(F32)
    for k in range(1, SEQ):
        summed += f_g[k].astype(F32)
    h_g[s] = (mid + summed).astype(BF16)
    spread(h_g.at[s], h_g, 15)
    renew(1, v_buf)
    store_values = pltpu.make_async_copy(v_buf, out_values, store_sem.at[1])
    store_values.start()

    for buf, phase in ((wq_g, 0), (wkvo_g, 2), (wu_g, 6), (wd_g, 8)):
        sent(buf.at[pl.ds(0, 3)], phase)
        sent(buf.at[pl.ds(0, 4)], phase + 1)
    for buf, phase in ((q_g, 4), (p_g, 10), (a_g, 12), (o_g, 13), (f_g, 14)):
        sent(buf.at[pl.ds(0, SEQ - 1)], phase)
    sent(kv_g.at[0, pl.ds(0, 7)], 5)
    sent(kv_g.at[pl.ds(0, 3)], 16)
    sent(kv_p, 11)
    received(h_g.at[pl.ds(0, SEQ - 1)], 15)
    for j in range(HEADS):
        whole = jnp.concatenate([h_g[2 * j], h_g[2 * j + 1]], axis=0).astype(F32)
        for i in range(8):
            out[i, :, 128 * j : 128 * j + 128] = whole[4 * i : 4 * i + 4].astype(BF16)
    sent(h_g.at[pl.ds(0, SEQ - 1)], 15)
    store_keys.wait()
    store_values.wait()


def finish(hidden, keys, values, out, out_keys, out_values, h_buf, k_buf, v_buf, in_sem, out_sem):
    half = SPOTS // 2
    moves = [(hidden, h_buf, out)]
    for a, b, c in ((keys, k_buf, out_keys), (values, v_buf, out_values)):
        for i in range(2):
            part = pl.ds(i * half, half)
            moves.append((a.at[part], b.at[part], c.at[part]))
    ins = [pltpu.make_async_copy(a, b, in_sem.at[i]) for i, (a, b, _) in enumerate(moves)]
    outs = [pltpu.make_async_copy(b, c, out_sem.at[i]) for i, (_, b, c) in enumerate(moves)]
    for copy in ins:
        copy.start()
    for arrived, copy in zip(ins, outs):
        arrived.wait()
        copy.start()
    for copy in outs:
        copy.wait()


def body(
    tokens,
    lengths,
    cache_keys,
    cache_values,
    norm1_gain,
    norm1_bias,
    w_query,
    b_query,
    w_key,
    b_key,
    w_value,
    b_value,
    w_out,
    b_out,
    norm2_gain,
    norm2_bias,
    w_up,
    b_up,
    w_down,
    b_down,
):
    vmem = pl.BlockSpec(memory_space=pltpu.VMEM)
    hbm = pl.BlockSpec(memory_space=pltpu.HBM)

    def line(v):
        return v.reshape(1, -1)

    slots = pltpu.VMEM((SEQ, 16, 128), BF16)
    hidden_out, new_keys, new_values = pl.pallas_call(
        kernel,
        out_shape=(
            jax.ShapeDtypeStruct((8, 4, WIDTH), BF16),
            jax.ShapeDtypeStruct((SPOTS, WIDTH), BF16),
            jax.ShapeDtypeStruct((SPOTS, WIDTH), BF16),
        ),
        in_specs=[hbm] * 20,
        out_specs=(vmem, hbm, hbm),
        scratch_shapes=[
            pltpu.VMEM((ROWS, WIDTH), F32),
            pltpu.VMEM((ROWS, WIDTH), BF16),
            pltpu.VMEM((SPOTS, WIDTH), BF16),
            pltpu.VMEM((SPOTS, WIDTH), BF16),
            pltpu.SMEM((8,), jnp.int32),
            pltpu.VMEM((8, 4, WIDTH), BF16),
            pltpu.VMEM((1, WIDTH), F32),
            pltpu.VMEM((1, WIDTH), F32),
            pltpu.VMEM((1, 64), F32),
            pltpu.VMEM((1, 64), F32),
            pltpu.VMEM((1, 64), F32),
            pltpu.VMEM((1, 64), F32),
            pltpu.VMEM((1, WIDTH), F32),
            pltpu.VMEM((1, WIDTH), F32),
            pltpu.VMEM((1, 256), F32),
            pltpu.VMEM((1, WIDTH), F32),
            pltpu.VMEM((REQ, 64, 256), BF16),
            pltpu.VMEM((REQ, 3, 64, 256), BF16),
            pltpu.VMEM((REQ, 256, 256), BF16),
            pltpu.VMEM((REQ, 256, 256), BF16),
            slots,
            pltpu.VMEM((4, 8, 2, 16, 128), BF16),
            pltpu.VMEM((2, 16, 128), BF16),
            pltpu.VMEM((SEQ, 32, 128), BF16),
            pltpu.VMEM((SEQ, 32, 128), BF16),
            slots,
            slots,
            slots,
            slots,
            slots,
            pltpu.SemaphoreType.DMA((20,)),
            pltpu.SemaphoreType.DMA((2,)),
            pltpu.SemaphoreType.DMA((17,)),
            pltpu.SemaphoreType.DMA((17,)),
            pltpu.SemaphoreType.DMA((SEQ,)),
            pltpu.SemaphoreType.REGULAR,
            pltpu.SemaphoreType.REGULAR,
        ],
        compiler_params=pltpu.CompilerParams(
            collective_id=0, has_side_effects=True, vmem_limit_bytes=58 * 1024 * 1024
        ),
        cost_estimate=pl.CostEstimate(flops=500_000_000, bytes_accessed=9_000_000, transcendentals=300_000),
    )(
        lengths,
        tokens,
        cache_keys.reshape(SPOTS, WIDTH),
        cache_values.reshape(SPOTS, WIDTH),
        line(norm1_gain),
        line(norm1_bias),
        w_query.T,
        line(b_query),
        w_key.T,
        line(b_key),
        w_value.T,
        line(b_value),
        w_out.T,
        line(b_out),
        line(norm2_gain),
        line(norm2_bias),
        w_up,
        line(b_up),
        w_down,
        line(b_down),
    )
    hidden_out, new_keys, new_values = pl.pallas_call(
        finish,
        out_shape=(
            jax.ShapeDtypeStruct((8, 4, WIDTH), BF16),
            jax.ShapeDtypeStruct((SPOTS, WIDTH), BF16),
            jax.ShapeDtypeStruct((SPOTS, WIDTH), BF16),
        ),
        in_specs=[hbm] * 3,
        out_specs=(hbm, hbm, hbm),
        scratch_shapes=[
            pltpu.VMEM((8, 4, WIDTH), BF16),
            pltpu.VMEM((SPOTS, WIDTH), BF16),
            pltpu.VMEM((SPOTS, WIDTH), BF16),
            pltpu.SemaphoreType.DMA((5,)),
            pltpu.SemaphoreType.DMA((5,)),
        ],
        compiler_params=pltpu.CompilerParams(vmem_limit_bytes=58 * 1024 * 1024),
    )(hidden_out, new_keys, new_values)
    return hidden_out, new_keys.reshape(8, 64, WIDTH), new_values.reshape(8, 64, WIDTH)


def solution(mesh):
    in_specs = (
        P("req", None, None),
        P("req"),
        P("req", "seq", None),
        P("req", "seq", None),
        P(),
        P(),
        P("req", "seq"),
        P("seq"),
        P("req", "seq"),
        P("seq"),
        P("req", "seq"),
        P("seq"),
        P("req", "seq"),
        P("seq"),
        P(),
        P(),
        P("req", "seq"),
        P("seq"),
        P("seq", "req"),
        P(),
    )
    out_specs = (P("req", None, None), P("req", "seq", None), P("req", "seq", None))
    return jax.shard_map(body, mesh=mesh, in_specs=in_specs, out_specs=out_specs, check_vma=False)
```

```python
import functools

import jax
import jax.numpy as jnp
from jax import lax
from jax.experimental import pallas as pl
from jax.experimental.pallas import tpu as pltpu
from jax.sharding import PartitionSpec as P

HEADS = 16
HEAD = 128
SEQ = 32
REQ = 8
ROWS = 32
WIDTH = 2048
SPOTS = 512
MESH = pl.DeviceIdType.MESH
F32 = jnp.float32
BF16 = jnp.bfloat16
NT = (((1,), (1,)), ((), ()))
ORDER = (
    ((0, 0), (0, 1), (1, 0), (7, 0)),
    ((1, 1), (7, 1), (2, 0), (6, 0)),
    ((4, 1), (4, 0), (3, 1), (5, 1)),
    ((3, 0), (5, 0), (2, 1), (6, 1)),
)


def layer_norm(values, gain, shift):
    center = values - jnp.mean(values, axis=-1, keepdims=True)
    spread = jnp.mean(center * center, axis=-1, keepdims=True)
    return center * lax.rsqrt(spread + 1e-05) * gain + shift


def hops(offset):
    dz, dx = offset
    return min(dz, 8 - dz) + min(dx, 4 - dx)


FAR = sorted(((dz, dx) for dz in range(8) for dx in range(4) if dz + dx), key=hops, reverse=True)


def unfold(slots, j):
    return unfold_pair(slots[2 * j], slots[2 * j + 1])


def unfold_pair(first, second):
    first, second = first.astype(F32), second.astype(F32)
    low = lax.broadcasted_iota(jnp.int32, (16, 128), 1) < 64
    top = jnp.where(low, first, pltpu.roll(second, 64, 1))
    bottom = jnp.where(low, pltpu.roll(first, 64, 1), second)
    return jnp.concatenate([top, bottom], axis=0)


def kernel(
    lengths,
    tokens,
    cache_keys,
    cache_values,
    gain1,
    bias1,
    wq,
    bq,
    wk,
    bk,
    wv,
    bv,
    wo,
    bo,
    gain2,
    bias2,
    wu,
    bu,
    wd,
    bd,
    out,
    out_keys,
    out_values,
    x_buf,
    n_buf,
    k_buf,
    v_buf,
    lengths_s,
    tokens_s,
    gain1_s,
    bias1_s,
    bq_s,
    bk_s,
    bv_s,
    bo_s,
    gain2_s,
    bias2_s,
    bu_s,
    bd_s,
    wq_g,
    wkvo_g,
    wu_g,
    wd_g,
    q_g,
    kv_g,
    kv_p,
    p_s,
    p_g,
    a_g,
    o_g,
    f_s,
    f_g,
    h_g,
    load_sem,
    store_sem,
    send_sem,
    recv_sem,
    query_sem,
    column_sem,
    plane_sem,
):
    s = lax.axis_index("seq")
    r = lax.axis_index("req")
    z, x = s // 4, lax.rem(s, 4)
    y, core = r // 2, lax.rem(r, 2)
    sibling = y * 2 + 1 - core
    head, half = s // 2, lax.rem(s, 2)
    partner = s + 1 - 2 * half

    barrier = pltpu.get_barrier_semaphore()

    def along(dz, dx):
        return (((z + dz) & 7) * 4 + ((x + dx) & 3), r)

    for dz, dx in ((2, 0), (6, 0), (0, 2), (1, 0), (7, 0), (0, 1), (0, 3)):
        pl.semaphore_signal(barrier, inc=1, device_id=along(dz, dx), device_id_type=MESH)
    for k in (4, 5, 2, 3, 6, 7, 1):
        near = lax.rem(y + k // 2, 4) * 2 + lax.rem(core + k, 2)
        pl.semaphore_signal(barrier, inc=1, device_id=(s, near), device_id_type=MESH)

    loads = [
        (tokens, tokens_s),
        (gain1, gain1_s),
        (bias1, bias1_s),
        (wq, wq_g.at[r]),
        (wk, wkvo_g.at[r, 0]),
        (wv, wkvo_g.at[r, 1]),
        (wo, wkvo_g.at[r, 2]),
        (bq, bq_s),
        (bk, bk_s),
        (bv, bv_s),
        (bo, bo_s),
        (lengths, lengths_s),
        (wu, wu_g.at[r]),
        (wd, wd_g.at[r]),
        (gain2, gain2_s),
        (bias2, bias2_s),
        (bu, bu_s),
        (bd, bd_s),
        (cache_keys, k_buf),
        (cache_values, v_buf),
    ]
    loads = [pltpu.make_async_copy(a, b, load_sem.at[i]) for i, (a, b) in enumerate(loads)]
    for load in loads:
        load.start()

    for load in loads[:3]:
        load.wait()
    for i in range(8):
        x_buf[4 * i : 4 * i + 4, :] = tokens_s[i].astype(F32)
    n_buf[...] = layer_norm(x_buf[...], gain1_s[...], bias1_s[...]).astype(BF16)

    def send(src, dst, phase, device):
        pltpu.make_async_remote_copy(
            src, dst, send_sem.at[phase], recv_sem.at[phase], device_id=device, device_id_type=MESH
        ).start()

    def received(ref, phase):
        pltpu.make_async_remote_copy(
            ref, ref, send_sem.at[phase], recv_sem.at[phase], device_id=(s, sibling), device_id_type=MESH
        ).wait_recv()

    def sent(ref, phase):
        pltpu.make_async_remote_copy(
            ref, ref, send_sem.at[phase], recv_sem.at[phase], device_id=(s, sibling), device_id_type=MESH
        ).wait_send()

    def spread(src, slots, phase):
        for offset in FAR:
            send(src, slots.at[s], phase, along(*offset))

    def along_y(buf, phase):
        for k in (2, 1, 3):
            send(buf.at[r], buf.at[r], phase, (s, lax.rem(y + k, 4) * 2 + core))

    def across(buf, phase, own):
        for k in (0,) if own else (1, 3, 2):
            block = lax.rem(y + k, 4) * 2 + core
            send(buf.at[block], buf.at[block], phase, (s, sibling))

    for load in loads[3:12]:
        load.wait()
    pl.semaphore_wait(barrier, 14)
    for dz in (2, 6):
        pl.semaphore_signal(column_sem, inc=1, device_id=along(dz, 0), device_id_type=MESH)

    along_y(wq_g, 0)
    across(wq_g, 1, True)
    along_y(wkvo_g, 2)
    across(wkvo_g, 3, True)
    pl.semaphore_wait(column_sem, 2)
    for dx in (2, 1, 3):
        pl.semaphore_signal(plane_sem, inc=1, device_id=along(0, dx), device_id_type=MESH)
    received(wq_g.at[pl.ds(0, 3)], 0)
    across(wq_g, 1, False)
    received(wq_g.at[pl.ds(0, 4)], 1)

    low = lax.broadcasted_iota(jnp.int32, (16, 128), 1) < 64

    total = jnp.zeros((ROWS, 128), F32)
    for k in range(REQ):
        weight = wq_g[k]
        total += lax.dot_general(
            n_buf[:, 256 * k : 256 * k + 256],
            jnp.concatenate([weight, weight], axis=0),
            NT,
            preferred_element_type=F32,
        )
    total += jnp.concatenate([bq_s[...], bq_s[...]], axis=1)
    q_g[s] = jnp.where(low, total[:16], total[16:]).astype(BF16)

    pl.semaphore_wait(plane_sem, 3)

    for offset in FAR:
        pltpu.make_async_remote_copy(
            q_g.at[s],
            q_g.at[s],
            send_sem.at[4],
            query_sem.at[s],
            device_id=along(*offset),
            device_id_type=MESH,
        ).start()

    received(wkvo_g.at[pl.ds(0, 3)], 2)
    across(wkvo_g, 3, False)
    for load in loads[12:]:
        load.wait()

    along_y(wu_g, 6)
    across(wu_g, 7, True)
    along_y(wd_g, 8)
    across(wd_g, 9, True)

    scale = HEAD**-0.5
    row = lax.broadcasted_iota(jnp.int32, (ROWS, SPOTS), 0)
    col = lax.broadcasted_iota(jnp.int32, (ROWS, SPOTS), 1)
    limit = jnp.zeros((ROWS, SPOTS), jnp.int32)
    for k in range(8):
        limit = jnp.where((row >> 2) == k, lengths_s[k], limit)
    valid = ((row >> 2) == (col >> 6)) & ((col & 63) + s * 64 < limit)
    lane = lax.broadcasted_iota(jnp.int32, (ROWS, 128), 1)
    marks = [lane == s + 32 * k for k in range(4)]

    def halves(value):
        first = value.astype(BF16).astype(F32)
        return first, (value - first).astype(BF16).astype(F32)

    for group in ORDER:
        heads = [(lax.rem(z + dz, 8) * 2 + lax.rem(x // 2 + dp, 2), dz + dp == 0) for dz, dp in group]
        for j, own in heads:
            for peer in (partner,) if own else (2 * j, 2 * j + 1):
                pltpu.make_async_copy(q_g.at[peer], q_g.at[peer], query_sem.at[peer]).wait()
        columns = [pl.ds(pl.multiple_of(j * 128, 128), 128) for j, _ in heads]
        scores = [
            lax.dot_general(
                unfold(q_g, j).astype(BF16), k_buf[:, columns[k]], NT, preferred_element_type=F32
            )
            for k, (j, _) in enumerate(heads)
        ]
        scores = [jnp.where(valid, score * scale, -1e30) for score in scores]
        peaks = [halves(jnp.maximum(jnp.max(score, axis=1, keepdims=True), -1e20)) for score in scores]
        expos = [jnp.exp(score - (peak[0] + peak[1])) for score, peak in zip(scores, peaks)]
        amounts = [halves(jnp.sum(expo, axis=1, keepdims=True)) for expo in expos]
        parts = [
            jnp.dot(expo.astype(BF16), v_buf[:, column], preferred_element_type=F32).astype(BF16)
            for expo, column in zip(expos, columns)
        ]
        for k, (j, own) in enumerate(heads):
            stats = jnp.zeros((ROWS, 128), F32)
            for mark, value in zip(marks, peaks[k] + amounts[k]):
                stats = jnp.where(mark, value, stats)
            stats = stats.astype(BF16)
            p_s[2 * j, 0:16] = parts[k][:16]
            p_s[2 * j, 16:32] = stats[:16]
            p_s[2 * j + 1, 0:16] = parts[k][16:]
            p_s[2 * j + 1, 16:32] = stats[16:]
            for peer in (partner,) if own else (2 * j, 2 * j + 1):
                send(p_s.at[peer], p_g.at[s], 10, (peer, r))
    p_g[s] = p_s[s]

    received(wkvo_g.at[pl.ds(0, 4)], 3)
    total = jnp.zeros((ROWS, 128), F32)
    for k in range(REQ):
        total += lax.dot_general(
            n_buf[:, 256 * k : 256 * k + 256],
            wkvo_g[k, 0:2].reshape(128, 256),
            NT,
            preferred_element_type=F32,
        )
    total += jnp.concatenate([bk_s[...], bv_s[...]], axis=1)
    kv_g[x, z, 0] = jnp.where(low, total[:16], pltpu.roll(total[16:], 64, 1)).astype(BF16)
    kv_g[x, z, 1] = jnp.where(low, pltpu.roll(total[:16], 64, 1), total[16:]).astype(BF16)
    send(kv_g.at[x, z], kv_p, 11, (partner, r))

    def mine(which):
        own, other = kv_g[x, z, which].astype(F32), kv_p[which].astype(F32)
        first, second = jnp.where(half == 0, own, other), jnp.where(half == 0, other, own)
        return unfold_pair(first, second).astype(BF16)

    received(kv_p, 11)
    query = unfold(q_g, head)
    query = jnp.where(half == 0, query[:16], query[16:]).astype(BF16)
    fresh_keys = mine(0)
    fresh_values = mine(1)
    row = lax.broadcasted_iota(jnp.int32, (16, ROWS), 0) + half * 16
    col = lax.broadcasted_iota(jnp.int32, (16, ROWS), 1)
    scores = lax.dot_general(query, fresh_keys, NT, preferred_element_type=F32) * scale
    scores = jnp.where(((row >> 2) == (col >> 2)) & ((col & 3) <= (row & 3)), scores, -1e30)
    peak_new = jnp.max(scores, axis=1, keepdims=True)
    expo = jnp.exp(scores - peak_new)
    total_new = jnp.sum(expo, axis=1, keepdims=True)
    part_new = jnp.dot(expo.astype(BF16), fresh_values, preferred_element_type=F32)

    received(p_g.at[pl.ds(0, SEQ - 1)], 10)
    stats = p_g[0, 16:32].astype(F32)
    for k in range(1, SEQ):
        stats += p_g[k, 16:32].astype(F32)
    stats += pltpu.roll(stats, 96, 1)
    lane = lax.broadcasted_iota(jnp.int32, (16, 128), 1)
    peaks = jnp.where(lane < 32, stats, -1e20)
    totals = jnp.where(lane < 32, pltpu.roll(stats, 64, 1), 0.0)
    peak = jnp.maximum(jnp.max(peaks, axis=1, keepdims=True), peak_new)
    share_new = jnp.exp(peak_new - peak)
    shares = jnp.exp(peaks - peak)
    total = jnp.sum(shares * totals, axis=1, keepdims=True) + share_new * total_new
    mixed = share_new * part_new
    for k in range(SEQ):
        mixed += shares[:, k : k + 1] * p_g[k, 0:16].astype(F32)
    a_g[s] = (mixed / total).astype(BF16)
    spread(a_g.at[s], a_g, 12)

    for dz in (4, 3, 5, 2, 6, 1, 7):
        send(kv_g.at[x, z], kv_g.at[x, z], 5, along(dz, 0))

    received(wu_g.at[pl.ds(0, 3)], 6)
    across(wu_g, 7, False)
    received(wd_g.at[pl.ds(0, 3)], 8)
    across(wd_g, 9, False)
    received(a_g.at[pl.ds(0, SEQ - 1)], 12)
    total = jnp.zeros((ROWS, 128), F32)
    for k in range(REQ):
        left = jnp.concatenate([a_g[4 * k], a_g[4 * k + 1]], axis=0)
        right = jnp.concatenate([a_g[4 * k + 2], a_g[4 * k + 3]], axis=0)
        weight = wkvo_g[k, 2]
        total += lax.dot_general(
            jnp.concatenate([left, right], axis=1),
            jnp.concatenate([weight, weight], axis=0),
            NT,
            preferred_element_type=F32,
        )
    total += jnp.concatenate([bo_s[...], bo_s[...]], axis=1)
    o_g[s] = jnp.where(low, total[:16], total[16:]).astype(BF16)
    spread(o_g.at[s], o_g, 13)
    received(kv_g.at[0, pl.ds(0, 7)], 5)
    for dx in (2, 1, 3):
        send(kv_g.at[x], kv_g.at[x], 16, along(0, dx))

    received(wu_g.at[pl.ds(0, 4)], 7)
    received(wd_g.at[pl.ds(0, 4)], 9)
    received(o_g.at[pl.ds(0, SEQ - 1)], 13)

    for j in range(HEADS):
        x_buf[:, 128 * j : 128 * j + 128] += unfold(o_g, j)
    n_buf[...] = layer_norm(x_buf[...], gain2_s[...], bias2_s[...]).astype(BF16)
    total = jnp.zeros((ROWS, 256), F32)
    for k in range(REQ):
        total += jnp.dot(n_buf[:, 256 * k : 256 * k + 256], wu_g[k], preferred_element_type=F32)
    total += bu_s[...]
    hidden = (0.5 * total * (1.0 + lax.erf(total * (0.5**0.5)))).astype(BF16)
    for k in range(REQ):
        feed = jnp.dot(hidden, wd_g[k], preferred_element_type=F32).astype(BF16)
        f_s[4 * k] = feed[:16, :128]
        f_s[4 * k + 1] = feed[16:, :128]
        f_s[4 * k + 2] = feed[:16, 128:]
        f_s[4 * k + 3] = feed[16:, 128:]

    for offset in FAR:
        peer = along(*offset)
        send(f_s.at[peer[0]], f_g.at[s], 14, peer)
    f_g[s] = f_s[s]

    received(kv_g.at[pl.ds(0, 3)], 16)
    spot = lax.broadcasted_iota(jnp.int32, (SPOTS, ROWS), 0)
    new = lax.broadcasted_iota(jnp.int32, (SPOTS, ROWS), 1)
    start = jnp.zeros((SPOTS, ROWS), jnp.int32)
    for k in range(8):
        start = jnp.where((new >> 2) == k, lengths_s[k], start)
    hit = ((new >> 2) == (spot >> 6)) & ((spot & 63) + s * 64 == start + (new & 3))
    pick = jnp.where(hit, 1.0, 0.0)
    changed = jnp.max(pick, axis=1, keepdims=True) > 0.5
    pick = pick.astype(BF16)

    def renew(which, buf):
        def four(g, _):
            columns = [pl.ds(pl.multiple_of((4 * g + j) * 128, 128), 128) for j in range(4)]
            rows = [
                unfold_pair(
                    kv_g[2 * (j % 2), 2 * g + j // 2, which], kv_g[2 * (j % 2) + 1, 2 * g + j // 2, which]
                ).astype(BF16)
                for j in range(4)
            ]
            fresh = [jnp.dot(pick, row, preferred_element_type=F32) for row in rows]
            for j in range(4):
                old = buf[:, columns[j]].astype(F32)
                buf[:, columns[j]] = jnp.where(changed, fresh[j], old).astype(BF16)
            return 0

        lax.fori_loop(0, HEADS // 4, four, 0)

    renew(0, k_buf)
    store_keys = pltpu.make_async_copy(k_buf, out_keys, store_sem.at[0])
    store_keys.start()

    columns = pl.ds(pl.multiple_of(head * 128, 128), 128)
    mid = x_buf[pl.ds(pl.multiple_of(half * 16, 16), 16), columns] + bd_s[:, columns]
    received(f_g.at[pl.ds(0, SEQ - 1)], 14)
    summed = f_g[0].astype(F32)
    for k in range(1, SEQ):
        summed += f_g[k].astype(F32)
    h_g[s] = (mid + summed).astype(BF16)
    spread(h_g.at[s], h_g, 15)
    renew(1, v_buf)
    store_values = pltpu.make_async_copy(v_buf, out_values, store_sem.at[1])
    store_values.start()

    for buf, phase in ((wq_g, 0), (wkvo_g, 2), (wu_g, 6), (wd_g, 8)):
        sent(buf.at[pl.ds(0, 3)], phase)
        sent(buf.at[pl.ds(0, 4)], phase + 1)
    for buf, phase in ((q_g, 4), (p_g, 10), (a_g, 12), (o_g, 13), (f_g, 14)):
        sent(buf.at[pl.ds(0, SEQ - 1)], phase)
    sent(kv_g.at[0, pl.ds(0, 7)], 5)
    sent(kv_g.at[pl.ds(0, 3)], 16)
    sent(kv_p, 11)
    received(h_g.at[pl.ds(0, SEQ - 1)], 15)
    for j in range(HEADS):
        whole = jnp.concatenate([h_g[2 * j], h_g[2 * j + 1]], axis=0).astype(F32)
        for i in range(8):
            out[i, :, 128 * j : 128 * j + 128] = whole[4 * i : 4 * i + 4].astype(BF16)
    sent(h_g.at[pl.ds(0, SEQ - 1)], 15)
    store_keys.wait()
    store_values.wait()


def finish(hidden, keys, values, out, out_keys, out_values, h_buf, k_buf, v_buf, in_sem, out_sem):
    half = SPOTS // 2
    moves = [(hidden, h_buf, out)]
    for a, b, c in ((keys, k_buf, out_keys), (values, v_buf, out_values)):
        for i in range(2):
            part = pl.ds(i * half, half)
            moves.append((a.at[part], b.at[part], c.at[part]))
    ins = [pltpu.make_async_copy(a, b, in_sem.at[i]) for i, (a, b, _) in enumerate(moves)]
    outs = [pltpu.make_async_copy(b, c, out_sem.at[i]) for i, (_, b, c) in enumerate(moves)]
    for copy in ins:
        copy.start()
    for arrived, copy in zip(ins, outs):
        arrived.wait()
        copy.start()
    for copy in outs:
        copy.wait()


def body(
    tokens,
    lengths,
    cache_keys,
    cache_values,
    norm1_gain,
    norm1_bias,
    w_query,
    b_query,
    w_key,
    b_key,
    w_value,
    b_value,
    w_out,
    b_out,
    norm2_gain,
    norm2_bias,
    w_up,
    b_up,
    w_down,
    b_down,
):
    vmem = pl.BlockSpec(memory_space=pltpu.VMEM)
    hbm = pl.BlockSpec(memory_space=pltpu.HBM)

    def line(v):
        return v.reshape(1, -1)

    slots = pltpu.VMEM((SEQ, 16, 128), BF16)
    hidden_out, new_keys, new_values = pl.pallas_call(
        kernel,
        out_shape=(
            jax.ShapeDtypeStruct((8, 4, WIDTH), BF16),
            jax.ShapeDtypeStruct((SPOTS, WIDTH), BF16),
            jax.ShapeDtypeStruct((SPOTS, WIDTH), BF16),
        ),
        in_specs=[hbm] * 20,
        out_specs=(vmem, hbm, hbm),
        scratch_shapes=[
            pltpu.VMEM((ROWS, WIDTH), F32),
            pltpu.VMEM((ROWS, WIDTH), BF16),
            pltpu.VMEM((SPOTS, WIDTH), BF16),
            pltpu.VMEM((SPOTS, WIDTH), BF16),
            pltpu.SMEM((8,), jnp.int32),
            pltpu.VMEM((8, 4, WIDTH), BF16),
            pltpu.VMEM((1, WIDTH), F32),
            pltpu.VMEM((1, WIDTH), F32),
            pltpu.VMEM((1, 64), F32),
            pltpu.VMEM((1, 64), F32),
            pltpu.VMEM((1, 64), F32),
            pltpu.VMEM((1, 64), F32),
            pltpu.VMEM((1, WIDTH), F32),
            pltpu.VMEM((1, WIDTH), F32),
            pltpu.VMEM((1, 256), F32),
            pltpu.VMEM((1, WIDTH), F32),
            pltpu.VMEM((REQ, 64, 256), BF16),
            pltpu.VMEM((REQ, 3, 64, 256), BF16),
            pltpu.VMEM((REQ, 256, 256), BF16),
            pltpu.VMEM((REQ, 256, 256), BF16),
            slots,
            pltpu.VMEM((4, 8, 2, 16, 128), BF16),
            pltpu.VMEM((2, 16, 128), BF16),
            pltpu.VMEM((SEQ, 32, 128), BF16),
            pltpu.VMEM((SEQ, 32, 128), BF16),
            slots,
            slots,
            slots,
            slots,
            slots,
            pltpu.SemaphoreType.DMA((20,)),
            pltpu.SemaphoreType.DMA((2,)),
            pltpu.SemaphoreType.DMA((17,)),
            pltpu.SemaphoreType.DMA((17,)),
            pltpu.SemaphoreType.DMA((SEQ,)),
            pltpu.SemaphoreType.REGULAR,
            pltpu.SemaphoreType.REGULAR,
        ],
        compiler_params=pltpu.CompilerParams(
            collective_id=0, has_side_effects=True, vmem_limit_bytes=58 * 1024 * 1024
        ),
        cost_estimate=pl.CostEstimate(flops=500_000_000, bytes_accessed=9_000_000, transcendentals=300_000),
    )(
        lengths,
        tokens,
        cache_keys.reshape(SPOTS, WIDTH),
        cache_values.reshape(SPOTS, WIDTH),
        line(norm1_gain),
        line(norm1_bias),
        w_query.T,
        line(b_query),
        w_key.T,
        line(b_key),
        w_value.T,
        line(b_value),
        w_out.T,
        line(b_out),
        line(norm2_gain),
        line(norm2_bias),
        w_up,
        line(b_up),
        w_down,
        line(b_down),
    )
    hidden_out, new_keys, new_values = pl.pallas_call(
        finish,
        out_shape=(
            jax.ShapeDtypeStruct((8, 4, WIDTH), BF16),
            jax.ShapeDtypeStruct((SPOTS, WIDTH), BF16),
            jax.ShapeDtypeStruct((SPOTS, WIDTH), BF16),
        ),
        in_specs=[hbm] * 3,
        out_specs=(hbm, hbm, hbm),
        scratch_shapes=[
            pltpu.VMEM((8, 4, WIDTH), BF16),
            pltpu.VMEM((SPOTS, WIDTH), BF16),
            pltpu.VMEM((SPOTS, WIDTH), BF16),
            pltpu.SemaphoreType.DMA((5,)),
            pltpu.SemaphoreType.DMA((5,)),
        ],
        compiler_params=pltpu.CompilerParams(vmem_limit_bytes=58 * 1024 * 1024),
    )(hidden_out, new_keys, new_values)
    return hidden_out, new_keys.reshape(8, 64, WIDTH), new_values.reshape(8, 64, WIDTH)


def solution(mesh):
    in_specs = (
        P("req", None, None),
        P("req"),
        P("req", "seq", None),
        P("req", "seq", None),
        P(),
        P(),
        P("req", "seq"),
        P("seq"),
        P("req", "seq"),
        P("seq"),
        P("req", "seq"),
        P("seq"),
        P("req", "seq"),
        P("seq"),
        P(),
        P(),
        P("req", "seq"),
        P("seq"),
        P("seq", "req"),
        P(),
    )
    out_specs = (P("req", None, None), P("req", "seq", None), P("req", "seq", None))
    return jax.shard_map(body, mesh=mesh, in_specs=in_specs, out_specs=out_specs, check_vma=False)
```

```python
import functools

import jax
import jax.numpy as jnp
from jax import lax
from jax.experimental import pallas as pl
from jax.experimental.pallas import tpu as pltpu
from jax.sharding import PartitionSpec as P

HEADS = 16
HEAD = 128
SEQ = 32
REQ = 8
ROWS = 32
WIDTH = 2048
SPOTS = 512
MESH = pl.DeviceIdType.MESH
F32 = jnp.float32
BF16 = jnp.bfloat16
NT = (((1,), (1,)), ((), ()))
ORDER = (
    ((0, 0), (0, 1), (1, 0), (7, 0)),
    ((1, 1), (7, 1), (2, 0), (6, 0)),
    ((4, 1), (4, 0), (3, 1), (5, 1)),
    ((3, 0), (5, 0), (2, 1), (6, 1)),
)


def layer_norm(values, gain, shift):
    center = values - jnp.mean(values, axis=-1, keepdims=True)
    spread = jnp.mean(center * center, axis=-1, keepdims=True)
    return center * lax.rsqrt(spread + 1e-05) * gain + shift


def hops(offset):
    dz, dx = offset
    return min(dz, 8 - dz) + min(dx, 4 - dx)


FAR = sorted(((dz, dx) for dz in range(8) for dx in range(4) if dz + dx), key=hops, reverse=True)


def unfold(slots, j):
    return unfold_pair(slots[2 * j], slots[2 * j + 1])


def unfold_pair(first, second):
    first, second = first.astype(F32), second.astype(F32)
    low = lax.broadcasted_iota(jnp.int32, (16, 128), 1) < 64
    top = jnp.where(low, first, pltpu.roll(second, 64, 1))
    bottom = jnp.where(low, pltpu.roll(first, 64, 1), second)
    return jnp.concatenate([top, bottom], axis=0)


def kernel(
    lengths,
    tokens,
    cache_keys,
    cache_values,
    gain1,
    bias1,
    wq,
    bq,
    wk,
    bk,
    wv,
    bv,
    wo,
    bo,
    gain2,
    bias2,
    wu,
    bu,
    wd,
    bd,
    out,
    out_keys,
    out_values,
    x_buf,
    n_buf,
    k_buf,
    v_buf,
    lengths_s,
    tokens_s,
    gain1_s,
    bias1_s,
    bq_s,
    bk_s,
    bv_s,
    bo_s,
    gain2_s,
    bias2_s,
    bu_s,
    bd_s,
    wq_g,
    wkvo_g,
    wu_g,
    wd_g,
    q_g,
    kv_g,
    kv_p,
    p_s,
    p_g,
    a_g,
    o_g,
    f_s,
    f_g,
    h_g,
    load_sem,
    store_sem,
    send_sem,
    recv_sem,
    query_sem,
    column_sem,
    plane_sem,
):
    s = lax.axis_index("seq")
    r = lax.axis_index("req")
    z, x = s // 4, lax.rem(s, 4)
    y, core = r // 2, lax.rem(r, 2)
    sibling = y * 2 + 1 - core
    head, half = s // 2, lax.rem(s, 2)
    partner = s + 1 - 2 * half

    barrier = pltpu.get_barrier_semaphore()

    def along(dz, dx):
        return (((z + dz) & 7) * 4 + ((x + dx) & 3), r)

    for dz, dx in ((2, 0), (6, 0), (0, 2), (1, 0), (7, 0), (0, 1), (0, 3)):
        pl.semaphore_signal(barrier, inc=1, device_id=along(dz, dx), device_id_type=MESH)
    for k in (4, 5, 2, 3, 6, 7, 1):
        near = lax.rem(y + k // 2, 4) * 2 + lax.rem(core + k, 2)
        pl.semaphore_signal(barrier, inc=1, device_id=(s, near), device_id_type=MESH)

    loads = [
        (tokens, tokens_s),
        (gain1, gain1_s),
        (bias1, bias1_s),
        (wq, wq_g.at[r]),
        (wk, wkvo_g.at[r, 0]),
        (wv, wkvo_g.at[r, 1]),
        (wo, wkvo_g.at[r, 2]),
        (bq, bq_s),
        (bk, bk_s),
        (bv, bv_s),
        (bo, bo_s),
        (lengths, lengths_s),
        (wu, wu_g.at[r]),
        (wd, wd_g.at[r]),
        (gain2, gain2_s),
        (bias2, bias2_s),
        (bu, bu_s),
        (bd, bd_s),
        (cache_keys, k_buf),
        (cache_values, v_buf),
    ]
    loads = [pltpu.make_async_copy(a, b, load_sem.at[i]) for i, (a, b) in enumerate(loads)]
    for load in loads:
        load.start()

    for load in loads[:3]:
        load.wait()
    for i in range(8):
        x_buf[4 * i : 4 * i + 4, :] = tokens_s[i].astype(F32)
    n_buf[...] = layer_norm(x_buf[...], gain1_s[...], bias1_s[...]).astype(BF16)

    def send(src, dst, phase, device):
        pltpu.make_async_remote_copy(
            src, dst, send_sem.at[phase], recv_sem.at[phase], device_id=device, device_id_type=MESH
        ).start()

    def received(ref, phase):
        pltpu.make_async_remote_copy(
            ref, ref, send_sem.at[phase], recv_sem.at[phase], device_id=(s, sibling), device_id_type=MESH
        ).wait_recv()

    def sent(ref, phase):
        pltpu.make_async_remote_copy(
            ref, ref, send_sem.at[phase], recv_sem.at[phase], device_id=(s, sibling), device_id_type=MESH
        ).wait_send()

    def spread(src, slots, phase):
        for offset in FAR:
            send(src, slots.at[s], phase, along(*offset))

    def along_y(buf, phase):
        for k in (2, 1, 3):
            send(buf.at[r], buf.at[r], phase, (s, lax.rem(y + k, 4) * 2 + core))

    def across(buf, phase, own):
        for k in (0,) if own else (1, 3, 2):
            block = lax.rem(y + k, 4) * 2 + core
            send(buf.at[block], buf.at[block], phase, (s, sibling))

    for load in loads[3:12]:
        load.wait()
    pl.semaphore_wait(barrier, 14)
    for dz in (2, 6):
        pl.semaphore_signal(column_sem, inc=1, device_id=along(dz, 0), device_id_type=MESH)

    along_y(wq_g, 0)
    across(wq_g, 1, True)
    along_y(wkvo_g, 2)
    across(wkvo_g, 3, True)
    pl.semaphore_wait(column_sem, 2)
    for dx in (2, 1, 3):
        pl.semaphore_signal(plane_sem, inc=1, device_id=along(0, dx), device_id_type=MESH)
    received(wq_g.at[pl.ds(0, 3)], 0)
    across(wq_g, 1, False)
    received(wq_g.at[pl.ds(0, 4)], 1)

    low = lax.broadcasted_iota(jnp.int32, (16, 128), 1) < 64

    total = jnp.zeros((ROWS, 128), F32)
    for k in range(REQ):
        weight = wq_g[k]
        total += lax.dot_general(
            n_buf[:, 256 * k : 256 * k + 256],
            jnp.concatenate([weight, weight], axis=0),
            NT,
            preferred_element_type=F32,
        )
    total += jnp.concatenate([bq_s[...], bq_s[...]], axis=1)
    q_g[s] = jnp.where(low, total[:16], total[16:]).astype(BF16)

    pl.semaphore_wait(plane_sem, 3)

    for offset in FAR:
        pltpu.make_async_remote_copy(
            q_g.at[s],
            q_g.at[s],
            send_sem.at[4],
            query_sem.at[s],
            device_id=along(*offset),
            device_id_type=MESH,
        ).start()

    received(wkvo_g.at[pl.ds(0, 3)], 2)
    across(wkvo_g, 3, False)
    for load in loads[12:]:
        load.wait()

    along_y(wu_g, 6)
    across(wu_g, 7, True)
    along_y(wd_g, 8)
    across(wd_g, 9, True)

    scale = HEAD**-0.5
    row = lax.broadcasted_iota(jnp.int32, (ROWS, SPOTS), 0)
    col = lax.broadcasted_iota(jnp.int32, (ROWS, SPOTS), 1)
    limit = jnp.zeros((ROWS, SPOTS), jnp.int32)
    for k in range(8):
        limit = jnp.where((row >> 2) == k, lengths_s[k], limit)
    valid = ((row >> 2) == (col >> 6)) & ((col & 63) + s * 64 < limit)
    lane = lax.broadcasted_iota(jnp.int32, (ROWS, 128), 1)
    marks = [lane == s + 32 * k for k in range(4)]

    def halves(value):
        first = value.astype(BF16).astype(F32)
        return first, (value - first).astype(BF16).astype(F32)

    for group in ORDER:
        heads = [(lax.rem(z + dz, 8) * 2 + lax.rem(x // 2 + dp, 2), dz + dp == 0) for dz, dp in group]
        for j, own in heads:
            for peer in (partner,) if own else (2 * j, 2 * j + 1):
                pltpu.make_async_copy(q_g.at[peer], q_g.at[peer], query_sem.at[peer]).wait()
        columns = [pl.ds(pl.multiple_of(j * 128, 128), 128) for j, _ in heads]
        scores = [
            lax.dot_general(
                unfold(q_g, j).astype(BF16), k_buf[:, columns[k]], NT, preferred_element_type=F32
            )
            for k, (j, _) in enumerate(heads)
        ]
        scores = [jnp.where(valid, score * scale, -1e30) for score in scores]
        peaks = [halves(jnp.maximum(jnp.max(score, axis=1, keepdims=True), -1e20)) for score in scores]
        expos = [jnp.exp(score - (peak[0] + peak[1])) for score, peak in zip(scores, peaks)]
        amounts = [halves(jnp.sum(expo, axis=1, keepdims=True)) for expo in expos]
        parts = [
            jnp.dot(expo.astype(BF16), v_buf[:, column], preferred_element_type=F32).astype(BF16)
            for expo, column in zip(expos, columns)
        ]
        for k, (j, own) in enumerate(heads):
            stats = jnp.zeros((ROWS, 128), F32)
            for mark, value in zip(marks, peaks[k] + amounts[k]):
                stats = jnp.where(mark, value, stats)
            stats = stats.astype(BF16)
            p_s[2 * j, 0:16] = parts[k][:16]
            p_s[2 * j, 16:32] = stats[:16]
            p_s[2 * j + 1, 0:16] = parts[k][16:]
            p_s[2 * j + 1, 16:32] = stats[16:]
            for peer in (partner,) if own else (2 * j, 2 * j + 1):
                send(p_s.at[peer], p_g.at[s], 10, (peer, r))
    p_g[s] = p_s[s]

    received(wkvo_g.at[pl.ds(0, 4)], 3)
    total = jnp.zeros((ROWS, 128), F32)
    for k in range(REQ):
        total += lax.dot_general(
            n_buf[:, 256 * k : 256 * k + 256],
            wkvo_g[k, 0:2].reshape(128, 256),
            NT,
            preferred_element_type=F32,
        )
    total += jnp.concatenate([bk_s[...], bv_s[...]], axis=1)
    kv_g[x, z, 0] = jnp.where(low, total[:16], pltpu.roll(total[16:], 64, 1)).astype(BF16)
    kv_g[x, z, 1] = jnp.where(low, pltpu.roll(total[:16], 64, 1), total[16:]).astype(BF16)
    send(kv_g.at[x, z], kv_p, 11, (partner, r))

    def mine(which):
        own, other = kv_g[x, z, which].astype(F32), kv_p[which].astype(F32)
        first, second = jnp.where(half == 0, own, other), jnp.where(half == 0, other, own)
        return unfold_pair(first, second).astype(BF16)

    received(kv_p, 11)
    query = unfold(q_g, head)
    query = jnp.where(half == 0, query[:16], query[16:]).astype(BF16)
    fresh_keys = mine(0)
    fresh_values = mine(1)
    row = lax.broadcasted_iota(jnp.int32, (16, ROWS), 0) + half * 16
    col = lax.broadcasted_iota(jnp.int32, (16, ROWS), 1)
    scores = lax.dot_general(query, fresh_keys, NT, preferred_element_type=F32) * scale
    scores = jnp.where(((row >> 2) == (col >> 2)) & ((col & 3) <= (row & 3)), scores, -1e30)
    peak_new = jnp.max(scores, axis=1, keepdims=True)
    expo = jnp.exp(scores - peak_new)
    total_new = jnp.sum(expo, axis=1, keepdims=True)
    part_new = jnp.dot(expo.astype(BF16), fresh_values, preferred_element_type=F32)

    received(p_g.at[pl.ds(0, SEQ - 1)], 10)
    stats = p_g[0, 16:32].astype(F32)
    for k in range(1, SEQ):
        stats += p_g[k, 16:32].astype(F32)
    stats += pltpu.roll(stats, 96, 1)
    lane = lax.broadcasted_iota(jnp.int32, (16, 128), 1)
    peaks = jnp.where(lane < 32, stats, -1e20)
    totals = jnp.where(lane < 32, pltpu.roll(stats, 64, 1), 0.0)
    peak = jnp.maximum(jnp.max(peaks, axis=1, keepdims=True), peak_new)
    share_new = jnp.exp(peak_new - peak)
    shares = jnp.exp(peaks - peak)
    total = jnp.sum(shares * totals, axis=1, keepdims=True) + share_new * total_new
    mixed = share_new * part_new
    for k in range(SEQ):
        mixed += shares[:, k : k + 1] * p_g[k, 0:16].astype(F32)
    a_g[s] = (mixed / total).astype(BF16)
    spread(a_g.at[s], a_g, 12)

    for dz in (4, 3, 5, 2, 6, 1, 7):
        send(kv_g.at[x, z], kv_g.at[x, z], 5, along(dz, 0))

    received(wu_g.at[pl.ds(0, 3)], 6)
    across(wu_g, 7, False)
    received(wd_g.at[pl.ds(0, 3)], 8)
    across(wd_g, 9, False)
    received(a_g.at[pl.ds(0, SEQ - 1)], 12)
    total = jnp.zeros((ROWS, 128), F32)
    for k in range(REQ):
        left = jnp.concatenate([a_g[4 * k], a_g[4 * k + 1]], axis=0)
        right = jnp.concatenate([a_g[4 * k + 2], a_g[4 * k + 3]], axis=0)
        weight = wkvo_g[k, 2]
        total += lax.dot_general(
            jnp.concatenate([left, right], axis=1),
            jnp.concatenate([weight, weight], axis=0),
            NT,
            preferred_element_type=F32,
        )
    total += jnp.concatenate([bo_s[...], bo_s[...]], axis=1)
    o_g[s] = jnp.where(low, total[:16], total[16:]).astype(BF16)
    spread(o_g.at[s], o_g, 13)
    received(kv_g.at[0, pl.ds(0, 7)], 5)
    for dx in (2, 1, 3):
        send(kv_g.at[x], kv_g.at[x], 16, along(0, dx))

    received(wu_g.at[pl.ds(0, 4)], 7)
    received(wd_g.at[pl.ds(0, 4)], 9)
    received(o_g.at[pl.ds(0, SEQ - 1)], 13)

    for j in range(HEADS):
        x_buf[:, 128 * j : 128 * j + 128] += unfold(o_g, j)
    n_buf[...] = layer_norm(x_buf[...], gain2_s[...], bias2_s[...]).astype(BF16)
    total = jnp.zeros((ROWS, 256), F32)
    for k in range(REQ):
        total += jnp.dot(n_buf[:, 256 * k : 256 * k + 256], wu_g[k], preferred_element_type=F32)
    total += bu_s[...]
    hidden = (0.5 * total * (1.0 + lax.erf(total * (0.5**0.5)))).astype(BF16)
    for k in range(REQ):
        feed = jnp.dot(hidden, wd_g[k], preferred_element_type=F32).astype(BF16)
        f_s[4 * k] = feed[:16, :128]
        f_s[4 * k + 1] = feed[16:, :128]
        f_s[4 * k + 2] = feed[:16, 128:]
        f_s[4 * k + 3] = feed[16:, 128:]

    for offset in FAR:
        peer = along(*offset)
        send(f_s.at[peer[0]], f_g.at[s], 14, peer)
    f_g[s] = f_s[s]

    received(kv_g.at[pl.ds(0, 3)], 16)
    spot = lax.broadcasted_iota(jnp.int32, (SPOTS, ROWS), 0)
    new = lax.broadcasted_iota(jnp.int32, (SPOTS, ROWS), 1)
    start = jnp.zeros((SPOTS, ROWS), jnp.int32)
    for k in range(8):
        start = jnp.where((new >> 2) == k, lengths_s[k], start)
    hit = ((new >> 2) == (spot >> 6)) & ((spot & 63) + s * 64 == start + (new & 3))
    pick = jnp.where(hit, 1.0, 0.0)
    changed = jnp.max(pick, axis=1, keepdims=True) > 0.5
    pick = pick.astype(BF16)

    def renew(which, buf):
        def four(g, _):
            columns = [pl.ds(pl.multiple_of((4 * g + j) * 128, 128), 128) for j in range(4)]
            rows = [
                unfold_pair(
                    kv_g[2 * (j % 2), 2 * g + j // 2, which], kv_g[2 * (j % 2) + 1, 2 * g + j // 2, which]
                ).astype(BF16)
                for j in range(4)
            ]
            fresh = [jnp.dot(pick, row, preferred_element_type=F32) for row in rows]
            for j in range(4):
                old = buf[:, columns[j]].astype(F32)
                buf[:, columns[j]] = jnp.where(changed, fresh[j], old).astype(BF16)
            return 0

        lax.fori_loop(0, HEADS // 4, four, 0)

    renew(0, k_buf)
    store_keys = pltpu.make_async_copy(k_buf, out_keys, store_sem.at[0])
    store_keys.start()

    columns = pl.ds(pl.multiple_of(head * 128, 128), 128)
    mid = x_buf[pl.ds(pl.multiple_of(half * 16, 16), 16), columns] + bd_s[:, columns]
    received(f_g.at[pl.ds(0, SEQ - 1)], 14)
    summed = f_g[0].astype(F32)
    for k in range(1, SEQ):
        summed += f_g[k].astype(F32)
    h_g[s] = (mid + summed).astype(BF16)
    spread(h_g.at[s], h_g, 15)
    renew(1, v_buf)
    store_values = pltpu.make_async_copy(v_buf, out_values, store_sem.at[1])
    store_values.start()

    for buf, phase in ((wq_g, 0), (wkvo_g, 2), (wu_g, 6), (wd_g, 8)):
        sent(buf.at[pl.ds(0, 3)], phase)
        sent(buf.at[pl.ds(0, 4)], phase + 1)
    for buf, phase in ((q_g, 4), (p_g, 10), (a_g, 12), (o_g, 13), (f_g, 14)):
        sent(buf.at[pl.ds(0, SEQ - 1)], phase)
    sent(kv_g.at[0, pl.ds(0, 7)], 5)
    sent(kv_g.at[pl.ds(0, 3)], 16)
    sent(kv_p, 11)
    received(h_g.at[pl.ds(0, SEQ - 1)], 15)
    out[...] = h_g[...]
    sent(h_g.at[pl.ds(0, SEQ - 1)], 15)
    store_keys.wait()
    store_values.wait()


def finish(hidden, keys, values, out, out_keys, out_values, h_g, h_buf, k_buf, v_buf, in_sem, out_sem):
    half = SPOTS // 2
    moves = []
    for a, b, c in ((keys, k_buf, out_keys), (values, v_buf, out_values)):
        for i in range(2):
            part = pl.ds(i * half, half)
            moves.append((a.at[part], b.at[part], c.at[part]))
    arrive = pltpu.make_async_copy(hidden, h_g, in_sem.at[4])
    leave = pltpu.make_async_copy(h_buf, out, out_sem.at[4])
    arrive.start()
    ins = [pltpu.make_async_copy(a, b, in_sem.at[i]) for i, (a, b, _) in enumerate(moves)]
    outs = [pltpu.make_async_copy(b, c, out_sem.at[i]) for i, (_, b, c) in enumerate(moves)]
    for copy in ins:
        copy.start()
    arrive.wait()
    for j in range(HEADS):
        whole = jnp.concatenate([h_g[2 * j], h_g[2 * j + 1]], axis=0).astype(F32)
        for i in range(8):
            h_buf[i, :, 128 * j : 128 * j + 128] = whole[4 * i : 4 * i + 4].astype(BF16)
    leave.start()
    for arrived, copy in zip(ins, outs):
        arrived.wait()
        copy.start()
    leave.wait()
    for copy in outs:
        copy.wait()


def body(
    tokens,
    lengths,
    cache_keys,
    cache_values,
    norm1_gain,
    norm1_bias,
    w_query,
    b_query,
    w_key,
    b_key,
    w_value,
    b_value,
    w_out,
    b_out,
    norm2_gain,
    norm2_bias,
    w_up,
    b_up,
    w_down,
    b_down,
):
    vmem = pl.BlockSpec(memory_space=pltpu.VMEM)
    hbm = pl.BlockSpec(memory_space=pltpu.HBM)

    def line(v):
        return v.reshape(1, -1)

    slots = pltpu.VMEM((SEQ, 16, 128), BF16)
    hidden_out, new_keys, new_values = pl.pallas_call(
        kernel,
        out_shape=(
            jax.ShapeDtypeStruct((SEQ, 16, 128), BF16),
            jax.ShapeDtypeStruct((SPOTS, WIDTH), BF16),
            jax.ShapeDtypeStruct((SPOTS, WIDTH), BF16),
        ),
        in_specs=[hbm] * 20,
        out_specs=(vmem, hbm, hbm),
        scratch_shapes=[
            pltpu.VMEM((ROWS, WIDTH), F32),
            pltpu.VMEM((ROWS, WIDTH), BF16),
            pltpu.VMEM((SPOTS, WIDTH), BF16),
            pltpu.VMEM((SPOTS, WIDTH), BF16),
            pltpu.SMEM((8,), jnp.int32),
            pltpu.VMEM((8, 4, WIDTH), BF16),
            pltpu.VMEM((1, WIDTH), F32),
            pltpu.VMEM((1, WIDTH), F32),
            pltpu.VMEM((1, 64), F32),
            pltpu.VMEM((1, 64), F32),
            pltpu.VMEM((1, 64), F32),
            pltpu.VMEM((1, 64), F32),
            pltpu.VMEM((1, WIDTH), F32),
            pltpu.VMEM((1, WIDTH), F32),
            pltpu.VMEM((1, 256), F32),
            pltpu.VMEM((1, WIDTH), F32),
            pltpu.VMEM((REQ, 64, 256), BF16),
            pltpu.VMEM((REQ, 3, 64, 256), BF16),
            pltpu.VMEM((REQ, 256, 256), BF16),
            pltpu.VMEM((REQ, 256, 256), BF16),
            slots,
            pltpu.VMEM((4, 8, 2, 16, 128), BF16),
            pltpu.VMEM((2, 16, 128), BF16),
            pltpu.VMEM((SEQ, 32, 128), BF16),
            pltpu.VMEM((SEQ, 32, 128), BF16),
            slots,
            slots,
            slots,
            slots,
            slots,
            pltpu.SemaphoreType.DMA((20,)),
            pltpu.SemaphoreType.DMA((2,)),
            pltpu.SemaphoreType.DMA((17,)),
            pltpu.SemaphoreType.DMA((17,)),
            pltpu.SemaphoreType.DMA((SEQ,)),
            pltpu.SemaphoreType.REGULAR,
            pltpu.SemaphoreType.REGULAR,
        ],
        compiler_params=pltpu.CompilerParams(
            collective_id=0, has_side_effects=True, vmem_limit_bytes=58 * 1024 * 1024
        ),
        cost_estimate=pl.CostEstimate(flops=500_000_000, bytes_accessed=9_000_000, transcendentals=300_000),
    )(
        lengths,
        tokens,
        cache_keys.reshape(SPOTS, WIDTH),
        cache_values.reshape(SPOTS, WIDTH),
        line(norm1_gain),
        line(norm1_bias),
        w_query.T,
        line(b_query),
        w_key.T,
        line(b_key),
        w_value.T,
        line(b_value),
        w_out.T,
        line(b_out),
        line(norm2_gain),
        line(norm2_bias),
        w_up,
        line(b_up),
        w_down,
        line(b_down),
    )
    hidden_out, new_keys, new_values = pl.pallas_call(
        finish,
        out_shape=(
            jax.ShapeDtypeStruct((8, 4, WIDTH), BF16),
            jax.ShapeDtypeStruct((SPOTS, WIDTH), BF16),
            jax.ShapeDtypeStruct((SPOTS, WIDTH), BF16),
        ),
        in_specs=[hbm] * 3,
        out_specs=(hbm, hbm, hbm),
        scratch_shapes=[
            pltpu.VMEM((SEQ, 16, 128), BF16),
            pltpu.VMEM((8, 4, WIDTH), BF16),
            pltpu.VMEM((SPOTS, WIDTH), BF16),
            pltpu.VMEM((SPOTS, WIDTH), BF16),
            pltpu.SemaphoreType.DMA((5,)),
            pltpu.SemaphoreType.DMA((5,)),
        ],
        compiler_params=pltpu.CompilerParams(vmem_limit_bytes=58 * 1024 * 1024),
    )(hidden_out, new_keys, new_values)
    return hidden_out, new_keys.reshape(8, 64, WIDTH), new_values.reshape(8, 64, WIDTH)


def solution(mesh):
    in_specs = (
        P("req", None, None),
        P("req"),
        P("req", "seq", None),
        P("req", "seq", None),
        P(),
        P(),
        P("req", "seq"),
        P("seq"),
        P("req", "seq"),
        P("seq"),
        P("req", "seq"),
        P("seq"),
        P("req", "seq"),
        P("seq"),
        P(),
        P(),
        P("req", "seq"),
        P("seq"),
        P("seq", "req"),
        P(),
    )
    out_specs = (P("req", None, None), P("req", "seq", None), P("req", "seq", None))
    return jax.shard_map(body, mesh=mesh, in_specs=in_specs, out_specs=out_specs, check_vma=False)
```
